128 devices in a mesh: grp: 16 (over x, z), sub: 8 (over y, core).
Axes of the slice: x: 4, y: 4, z: 4, core: 2. Of those that a mesh axis runs over, the one named last changes fastest.
Arguments:
- tiles: float32 [32768, 64, 64], P(('grp', 'sub')), may hold values from -0.3 to 0.3
- owner: int32 [32768, 1], P(('grp', 'sub')), may hold values from 0 to 127; in each aligned block of 256 rows (0 to 255, 256 to 511, ...) at most 4 rows name the same one
- slot: int32 [32768], P(('grp', 'sub')), may hold values from 0 to 159
- nbr: int32 [4096, 5], P(('grp', 'sub')), may hold values from 0 to 4095, as said below
- shift: float32 [262144], P(('grp', 'sub')), may hold values from 1 to 10
- start: float32 [262144, 64], P(('grp', 'sub')), may hold values from -6 to 6
Outputs:
- basis: float32 [262144, 64], P(('grp', 'sub'))
- coarse: float32 [16, 64, 192], P('grp', 'sub')
The draws below stay inside these ranges and needn't reach their ends.
Inputs may be any that keep to these rules, and one draw needn't show every extreme that they name: nbr[r,0] = r; the other entries of a row are distinct, differ from r, and lie among the block rows of devices r // 32 - 1, r // 32, r // 32 + 1 taken cyclically. Among the 256 tiles of one device, at most 4 name the same owner.
All inputs are finite; a program needn't handle non-finite values.
Results may differ from the reference program's by a relative error of at most 0.00015.
Values sent between devices are 32-bit elements; how exact they have to be, the bound alone decides.
A program may use at most 448 MiB of HBM per device.

```python
import math
import jax
import jax.numpy as jnp
import numpy as np
from jax import lax

TS = 64
NV = 64
K = 5
BLK_DEV = 32
CAP = 4
ITERS = 2
TILE_DEV = 256
NBLK = 4096
NROWS = 262144
TILES = 32768
N_GRP = 16
N_SUB = 8
DEVICES = 128


def draw_nbr(key, part):
    key = jax.random.fold_in(key, 7)
    total = BLK_DEV * DEVICES
    keys = jax.random.split(key, total)
    choices_count = 3 * BLK_DEV - 1
    picks = jax.vmap(lambda sub_key: jax.random.permutation(sub_key, choices_count)[:K - 1])(keys)
    rows = jnp.arange(total, dtype=jnp.int32)
    device = rows // BLK_DEV
    own_pos = rows - (device - 1) * BLK_DEV
    shifted = jnp.where(picks >= own_pos[:, None], picks + 1, picks)
    blocks = ((device[:, None] - 1) * BLK_DEV + shifted) % total
    return jnp.concatenate([rows[:, None], blocks.astype(jnp.int32)], axis=1).astype(jnp.int32)


def plant(values, own_key, least, top_value):
    extent = values.shape
    place = [jax.random.randint(jax.random.fold_in(own_key, axis), (), 0, extent[axis]) for axis in range(len(extent))]
    values = values.at[tuple(place)].set(least)
    longest = extent.index(max(extent))
    place[longest] = (place[longest] + 1) % extent[longest]
    return values.at[tuple(place)].set(top_value)


def level_of(stream_key, extent, pieces, smallest, largest):
    level = 1.0
    for position, parts in pieces:
        draws = jax.random.uniform(jax.random.fold_in(jax.random.fold_in(stream_key, 6), position), (parts,), jnp.float32, smallest / len(pieces), largest / len(pieces))
        level = level * jnp.repeat(jnp.exp(draws), extent[position] // parts).reshape((-1,) + (1,) * (len(extent) - 1 - position))
    return level


def routed_block(stream_key, own, number, rows, amount, top, reach, slope):
    order = jax.random.permutation(stream_key, amount)
    packed, common = portions_of(amount, rows * top, reach, slope, True), portions_of(amount, rows * top, reach, slope, False)
    places = jnp.arange(amount)

    def named(sizes, rotation):
        used = int((sizes > 0).sum())
        fixed = max(1, used // 4)
        moved = fixed + (places - fixed + rotation * (used - fixed)) % max(1, amount - fixed)
        return jnp.zeros((amount,), jnp.int32).at[order[jnp.where(places < fixed, places, moved)]].set(jnp.asarray(sizes, jnp.int32))

    sizes = jnp.where(number % 4 == 0, named(packed, number // 4), named(common, number - number // 4 - 1))
    mixed = jax.random.permutation(jax.random.fold_in(own, 3), amount)
    donor, taker = mixed[0:amount // 2 * 2:2], mixed[1:amount // 2 * 2:2]
    slack = jnp.minimum(sizes[donor] - 1, reach - sizes[taker]) // 2
    slack = jnp.where((donor == order[0]) | (taker == order[0]) | (sizes[taker] == 0), 0, jnp.maximum(slack, 0))
    moved = jax.random.randint(jax.random.fold_in(own, 4), (amount // 2,), 0, 1 << 20) % (slack + 1)
    sizes = sizes.at[donor].add(-moved).at[taker].add(moved)
    members = jnp.searchsorted(jnp.cumsum(sizes), jnp.arange(rows * top), side="right").astype(jnp.int32)
    listing = members.reshape(top, rows).T
    listing = listing[jax.random.permutation(jax.random.fold_in(own, 1), rows)]
    rotation = jax.random.randint(jax.random.fold_in(own, 2), (rows, 1), 0, top)
    return jnp.take_along_axis(listing, (jnp.arange(top)[None, :] + rotation) % top, axis=1)


def portions_of(number_of, total, limit, skew, full):
    loads = [(1 << 20) // math.isqrt(standing ** skew) + 1 for standing in range(1, number_of + 1)]
    largest = limit if full else min(limit, max(-(-total // number_of), total * loads[0] // sum(loads)))
    least = 1 if total - largest >= number_of - 1 else 0
    given, surplus = [largest] + [least] * (number_of - 1), total - largest - least * (number_of - 1)
    while surplus > 0:
        candidates = [i for i in range(1, number_of) if given[i] < largest] or [i for i in range(1, number_of) if given[i] < limit]
        pool, budget = sum([loads[i] for i in candidates]), surplus
        for i in candidates:
            addition = min(limit - given[i], max(1, budget * loads[i] // pool), surplus)
            given[i] = given[i] + addition
            surplus = surplus - addition
    return np.array(given)


def noise(key, extent, spread, most, cuts=(), kind=jnp.bfloat16):
    loudness = level_of(key, extent, cuts, -0.22, 0.18) if cuts else 1.0
    result = jax.random.normal(key, extent, jnp.float32) * spread * loudness
    return jnp.minimum(jnp.maximum(result, -most), most).astype(kind)


def setup_inputs(seed: int = 0) -> dict:
    splits = jax.random.split(jax.random.key(seed), 7)
    tiles = noise(splits[0], (TILES, TS, TS), 0.04, 0.3, ((0, 128),), jnp.float32)
    owner_keys = jax.random.split(jax.random.fold_in(splits[1], 1), TILES // TILE_DEV)
    owner_turns = jax.random.permutation(jax.random.fold_in(splits[1], 3), TILES // TILE_DEV)
    owner = jax.vmap(lambda own, number: routed_block(jax.random.fold_in(splits[1], 2), own, number, TILE_DEV, DEVICES, 1, CAP, 2))(owner_keys, owner_turns).reshape((TILES, 1))
    slot = plant(jax.random.randint(splits[2], (TILES,), 0, BLK_DEV * K), jax.random.fold_in(splits[2], 1), 0, (BLK_DEV * K) - 1).astype(jnp.int32)
    nbr = draw_nbr(jax.random.fold_in(splits[6], 71), 0)
    shift = jnp.clip(jnp.exp(math.log(10.0) - 2.3025851 * jax.random.uniform(splits[4], (NROWS,), jnp.float32) ** level_of(splits[4], (NROWS,), ((0, 128),), -0.2, 0.2)), 1.0, 10.0)
    start = noise(splits[5], (NROWS, NV), 1.0, 6.0, ((0, 128),), jnp.float32)
    return dict(tiles=tiles, owner=owner, slot=slot, nbr=nbr, shift=shift, start=start)


def apply_op(assembled, basis, nbr):
    blocks = basis.reshape(NBLK, TS, NV)[nbr]
    return jnp.einsum('rkab,rkbc->rkac', assembled, blocks, precision=lax.Precision.HIGHEST)

def reference(tiles, owner, slot, nbr, shift, start):
    target = owner[:, 0] * (BLK_DEV * K) + slot
    assembled = jax.ops.segment_sum(tiles, target, num_segments=NBLK * K).reshape(NBLK, K, TS, TS)
    eye = jnp.eye(TS, dtype=jnp.float32)
    assembled = assembled.at[:, 0].add(eye[None] * shift.reshape(NBLK, TS)[:, None, :])
    basis = start
    for step in range(ITERS):
        product = apply_op(assembled, basis, nbr).sum(axis=1).reshape(NROWS, NV)
        gram = jnp.dot(product.T, product, precision=lax.Precision.HIGHEST) / NROWS
        factor = jnp.linalg.cholesky(gram)
        basis = lax.linalg.triangular_solve(factor, product, left_side=False, lower=True, transpose_a=True)
    mapped = apply_op(assembled, basis, nbr)
    inner = jnp.einsum('rai,rkac->rkic', basis.reshape(NBLK, TS, NV), mapped, precision=lax.Precision.HIGHEST)
    owner_dev = jnp.arange(NBLK, dtype=jnp.int32) // BLK_DEV
    offset = (nbr // BLK_DEV - owner_dev[:, None] + 1) % DEVICES
    onehot = (offset[..., None] == jnp.arange(3, dtype=jnp.int32)).astype(jnp.float32)
    per_row = jnp.einsum('rko,rkic->roic', onehot, inner, precision=lax.Precision.HIGHEST)
    per_dev = per_row.reshape(DEVICES, BLK_DEV, 3, NV, NV).sum(axis=1).reshape(N_GRP, N_SUB, 3, NV, NV)
    sub_idx = jnp.arange(N_SUB)[None, :, None, None]
    first = (sub_idx == 0).astype(jnp.float32)
    last = (sub_idx == N_SUB - 1).astype(jnp.float32)
    lower = first * per_dev[:, :, 0]
    middle = per_dev[:, :, 1] + (1.0 - first) * per_dev[:, :, 0] + (1.0 - last) * per_dev[:, :, 2]
    upper = last * per_dev[:, :, 2]
    term = jnp.concatenate([lower, middle, upper], axis=3).sum(axis=1)
    coarse = term * (N_GRP / NROWS)
    return (basis, coarse)
```

```python
import functools

import jax
import jax.numpy as jnp
from jax import lax
from jax.experimental import pallas as pl
from jax.experimental.pallas import tpu as pltpu
from jax.sharding import PartitionSpec as P

K = 5
CAP = 4
TS = 64
HALF = 32
LANES = 128
BLK = 32
ROWS = BLK * TS
PAIRS = ROWS // LANES
SLOTS = BLK * K
NT = (((1,), (1,)), ((), ()))
NN = (((1,), (0,)), ((), ()))
MESH = pl.DeviceIdType.MESH
F32 = jnp.float32
BF16 = jnp.bfloat16


def dot(a, b, dims):
    return lax.dot_general(a, b, dims, preferred_element_type=F32)


def roll(x):
    return pltpu.roll(x, TS, axis=1)


def low_lanes(shape):
    return lax.broadcasted_iota(jnp.int32, shape, 1) < TS


def split(x):
    hi = x.astype(BF16)
    lo = (x - hi.astype(F32)).astype(BF16)
    return jnp.concatenate([hi, lo], axis=0)


def fold(out):
    t = out[:TS] + out[TS:]
    return t + roll(t)


def spread(x):
    low = low_lanes(x.shape)
    r = roll(x)
    return jnp.where(low, x, r), jnp.where(low, r, x)


def pack(x):
    return jnp.where(low_lanes((HALF, LANES)), x[:HALF], x[HALF:])


def half_masks():
    low = low_lanes((1, LANES)).astype(F32)
    return low.astype(BF16), (1.0 - low).astype(BF16)


def blocks_of(stack_ref, lidx_ref, r):
    return [stack_ref[lidx_ref[r * K + k]] for k in range(K)]


def apply_row(stack_ref, lidx_ref, op_ref, r, masks):
    low, high = masks
    b = blocks_of(stack_ref, lidx_ref, r)
    left = jnp.concatenate([b[0] * low + b[1] * high, b[2] * low + b[3] * high, b[4]], axis=1)
    return fold(dot(left, op_ref[r], NT))


def route_kernel(place_ref, x_ref, out_ref, packed, sem):
    half = pl.program_id(0)
    for c in range(HALF):
        block = jnp.concatenate(
            [x_ref[0, pl.ds(c * TS, TS), :], x_ref[1, pl.ds(c * TS, TS), :]], axis=0
        )
        packed[pl.ds(c, LANES, stride=HALF), :] = block.T

    def send(t, carry):
        src = packed.at[pl.ds(pl.multiple_of(t * HALF, HALF), HALF)]
        at = pl.multiple_of(place_ref[half * LANES + t] * HALF, HALF)
        pltpu.make_async_copy(src, out_ref.at[pl.ds(at, HALF)], sem).start()
        return carry

    lax.fori_loop(0, LANES, send, 0, unroll=8)
    pltpu.make_async_copy(packed, out_ref.at[pl.ds(0, LANES * HALF)], sem).wait()


def route(place, x, cells):
    count = x.shape[2]
    return pl.pallas_call(
        route_kernel,
        out_shape=jax.ShapeDtypeStruct((cells * HALF, LANES), F32),
        grid_spec=pltpu.PrefetchScalarGridSpec(
            num_scalar_prefetch=1,
            grid=(count // LANES,),
            in_specs=[pl.BlockSpec((2, HALF * TS, LANES), lambda i, *_: (0, 0, i))],
            out_specs=pl.BlockSpec(memory_space=pl.ANY),
            scratch_shapes=[pltpu.VMEM((LANES * HALF, LANES), F32), pltpu.SemaphoreType.DMA],
        ),
        compiler_params=pltpu.CompilerParams(vmem_limit_bytes=24 << 20),
    )(place, x)


GROUP = 64


def assemble_kernel(
    slots_ref, lidx_ref, got_ref, shift_ref, left_ref, own_ref, right_ref,
    op_ref, x_ref, g_ref, total, stack, halves,
):
    step = pl.program_id(0)

    @pl.when(step == 0)
    def _():
        total[...] = jnp.zeros_like(total)

    def add(p, carry):
        at = pl.ds(pl.multiple_of(slots_ref[step * GROUP + p] * HALF, HALF), HALF)
        total[at] = total[at] + got_ref[pl.ds(pl.multiple_of(p * HALF, HALF), HALF)]
        return carry

    lax.fori_loop(0, GROUP, add, 0, unroll=4)

    @pl.when(step == pl.num_programs(0) - 1)
    def _():
        low = low_lanes((HALF, LANES))
        row = lax.broadcasted_iota(jnp.int32, (HALF, LANES), 0)
        lane = lax.broadcasted_iota(jnp.int32, (HALF, LANES), 1)
        on_diagonal = (lane % TS) == row + HALF * (lane // TS)

        def form(r, carry):
            t = [total[pl.ds(pl.multiple_of((r * K + k) * HALF, HALF), HALF)] for k in range(K)]
            t[0] = t[0] + jnp.where(on_diagonal, shift_ref[pl.ds(r, 1)], 0.0)
            for j in range(3):
                a = t[2 * j]
                b = t[2 * j + 1] if 2 * j + 1 < K else jnp.zeros_like(a)
                both = jnp.concatenate(
                    [jnp.where(low, a, roll(b)), jnp.where(low, roll(a), b)], axis=0
                )
                op_ref[r, :, pl.ds(j * LANES, LANES)] = split(both)
            return carry

        lax.fori_loop(0, BLK, form, 0, unroll=2)

        for part, ref in enumerate((left_ref, own_ref, right_ref)):
            def cut(q, carry, part=part, ref=ref):
                x = ref[:, pl.ds(pl.multiple_of(q * LANES, LANES), LANES)]
                even, odd = spread(x)
                stack[part * BLK + 2 * q] = split(even)
                stack[part * BLK + 2 * q + 1] = split(odd)
                return carry

            lax.fori_loop(0, PAIRS, cut, 0, unroll=2)

        masks = half_masks()

        def product(q, carry):
            even = apply_row(stack, lidx_ref, op_ref, 2 * q, masks)
            odd = apply_row(stack, lidx_ref, op_ref, 2 * q + 1, masks)
            x = jnp.where(low_lanes(even.shape), even, odd)
            at = pl.ds(pl.multiple_of(q * LANES, LANES), LANES)
            x_ref[:, at] = x
            halves[:, at] = split(x)
            return carry

        lax.fori_loop(0, PAIRS, product, 0, unroll=4)
        g_ref[...] = pack(fold(dot(halves[...], halves[...], NT)))


def assemble(slots, lidx, got, shift2, left, own, right):
    steps = slots.shape[0] // GROUP
    whole = lambda shape: pl.BlockSpec(shape, lambda i, *_: (0,) * len(shape))
    return pl.pallas_call(
        assemble_kernel,
        out_shape=(
            jax.ShapeDtypeStruct((BLK, 2 * TS, 3 * LANES), BF16),
            jax.ShapeDtypeStruct((TS, ROWS), F32),
            jax.ShapeDtypeStruct((HALF, LANES), F32),
        ),
        grid_spec=pltpu.PrefetchScalarGridSpec(
            num_scalar_prefetch=2,
            grid=(steps,),
            in_specs=[
                pl.BlockSpec((GROUP * HALF, LANES), lambda i, *_: (i, 0)),
                whole((BLK, LANES)),
                whole((TS, ROWS)),
                whole((TS, ROWS)),
                whole((TS, ROWS)),
            ],
            out_specs=(whole((BLK, 2 * TS, 3 * LANES)), whole((TS, ROWS)), whole((HALF, LANES))),
            scratch_shapes=[
                pltpu.VMEM(((SLOTS + 1) * HALF, LANES), F32),
                pltpu.VMEM((3 * BLK, 2 * TS, LANES), BF16),
                pltpu.VMEM((2 * TS, ROWS), BF16),
            ],
        ),
        compiler_params=pltpu.CompilerParams(vmem_limit_bytes=40 << 20),
    )(slots, lidx, got, shift2, left, own, right)


def inverse_factor(gram):
    lane = lax.broadcasted_iota(jnp.int32, (8, LANES), 1)
    row = lax.broadcasted_iota(jnp.int32, (8, LANES), 0)
    rolled = roll(gram)
    blocks = []
    for b in range(TS // 8):
        source = gram if b < 4 else rolled
        part = source[8 * (b % 4) : 8 * (b % 4) + 8]
        unit = (lane == row + (TS + 8 * b)).astype(F32)
        blocks.append(jnp.where(lane < TS, part, unit))
    pivots = [None] * (TS // 8)
    for j in range(TS):
        jb, js = j // 8, j % 8
        spreadcol = {
            b: jnp.broadcast_to(blocks[b][:, j : j + 1], (8, LANES)) for b in range(jb, TS // 8)
        }
        pivot = jnp.broadcast_to(spreadcol[jb][js : js + 1], (8, LANES))
        scaled = jnp.broadcast_to(blocks[jb][js : js + 1], (8, LANES)) * (1.0 / pivot)
        first = jnp.where(row == js, pivot, jnp.zeros_like(pivot))
        pivots[jb] = first if pivots[jb] is None else pivots[jb] + first
        for b in range(jb, TS // 8):
            col = spreadcol[b]
            if b == jb:
                col = jnp.where(row > js, col, 0.0)
            blocks[b] = blocks[b] - col * scaled
    a = jnp.concatenate([blk * lax.rsqrt(p) for blk, p in zip(blocks, pivots)], axis=0)
    return jnp.where(low_lanes(a.shape), roll(a), a)


def wide(inverse):
    hi = inverse.astype(BF16)
    lo = (inverse - hi.astype(F32)).astype(BF16)
    return jnp.concatenate([hi, lo], axis=1)


def times(inverse, x):
    return dot(inverse, jnp.concatenate([x, x], axis=0), NN)


def iterate_kernel(
    groups, members, total_rows,
    lidx_ref, op_ref, x1_ref, g1_ref,
    basis_ref, coarse_ref,
    stack, halo1, halo2, z, halves, mapped, sub_got, grp_got, partial, final, term, tail,
    halo_send, halo_recv, sub_send, sub_recv, grp_send, grp_recv, term_send, term_recv,
):
    g, s = lax.axis_index("grp"), lax.axis_index("sub")
    me = g * members + s
    count = groups * members
    after, before = lax.rem(me + 1, count), lax.rem(me + count - 1, count)

    def device(index):
        return (index // members, lax.rem(index, members))

    subs = [(g, lax.rem(s + i, members)) for i in range(1, members)]
    grps = [(lax.rem(g + i, groups), s) for i in range(1, groups)]

    barrier = pltpu.get_barrier_semaphore()
    for peer in [device(after), device(before)] + subs + grps:
        pl.semaphore_signal(barrier, inc=1, device_id=peer, device_id_type=MESH)
    pl.semaphore_wait(barrier, 2 + len(subs) + len(grps))

    def remote(src, dst, send, recv, peer):
        return pltpu.make_async_remote_copy(
            src_ref=src, dst_ref=dst, send_sem=send, recv_sem=recv,
            device_id=peer, device_id_type=MESH,
        )

    def send_halo(src, halo, n):
        copies = [
            remote(src, halo.at[0], halo_send.at[n, 0], halo_recv.at[n, 0], device(after)),
            remote(src, halo.at[1], halo_send.at[n, 1], halo_recv.at[n, 1], device(before)),
        ]
        for c in copies:
            c.start()
        return copies

    def send_sub(src, got, sends, recvs, n):
        copies = [
            remote(src, got.at[n, s], sends.at[n, i], recvs.at[n, i], peer)
            for i, peer in enumerate(subs)
        ]
        for c in copies:
            c.start()
        return copies

    def send_grp(src, n):
        copies = [
            remote(src, grp_got.at[n, g], grp_send.at[n, i], grp_recv.at[n, i], peer)
            for i, peer in enumerate(grps)
        ]
        for c in copies:
            c.start()
        return copies

    def take(copies):
        for c in copies:
            c.wait_recv()

    def sum_sub(n):
        acc = sub_got[n, 0]
        for i in range(1, members):
            acc = acc + sub_got[n, i]
        return acc

    def sum_grp(n):
        acc = grp_got[n, 0]
        for i in range(1, groups):
            acc = acc + grp_got[n, i]
        return acc

    def columns(q):
        return pl.ds(pl.multiple_of(q * LANES, LANES), LANES)

    def put_pair(base, q, x):
        even, odd = spread(x)
        stack[base + 2 * q] = split(even)
        stack[base + 2 * q + 1] = split(odd)

    started = []

    first = send_sub(g1_ref, sub_got, sub_send, sub_recv, 0)
    sub_got[0, s] = g1_ref[...]
    halo = send_halo(x1_ref, halo1, 0)

    def own1(q, carry):
        put_pair(BLK, q, x1_ref[:, columns(q)])
        return carry

    lax.fori_loop(0, PAIRS, own1, 0, unroll=2)
    take(first)
    partial[0] = sum_sub(0)
    grp_got[0, g] = partial[0]
    second = send_grp(partial.at[0], 0)
    take(halo)
    started += first + halo + second

    for side in range(2):
        def ext1(q, carry, side=side):
            put_pair(side * 2 * BLK, q, halo1[side, :, columns(q)])
            return carry

        lax.fori_loop(0, PAIRS, ext1, 0, unroll=2)

    masks = half_masks()

    def product(q, carry):
        even = apply_row(stack, lidx_ref, op_ref, 2 * q, masks)
        odd = apply_row(stack, lidx_ref, op_ref, 2 * q + 1, masks)
        z[:, columns(q)] = jnp.where(low_lanes(even.shape), even, odd)
        return carry

    lax.fori_loop(0, PAIRS, product, 0, unroll=4)
    halo = send_halo(z, halo2, 1)
    started += halo

    take(second)
    inverse1 = wide(inverse_factor(sum_grp(0) / total_rows))

    def own2(q, carry):
        x = times(inverse1, split(z[:, columns(q)]))
        halves[:, columns(q)] = split(x)
        put_pair(BLK, q, x)
        return carry

    lax.fori_loop(0, PAIRS, own2, 0, unroll=4)
    partial[1] = pack(fold(dot(halves[...], halves[...], NT)))
    first = send_sub(partial.at[1], sub_got, sub_send, sub_recv, 1)
    sub_got[1, s] = partial[1]

    take(halo)
    for side in range(2):
        def ext2(q, carry, side=side):
            x = times(inverse1, split(halo2[side, :, columns(q)]))
            put_pair(side * 2 * BLK, q, x)
            return carry

        lax.fori_loop(0, PAIRS, ext2, 0, unroll=4)

    take(first)
    partial[2] = sum_sub(1)
    grp_got[1, g] = partial[2]
    second = send_grp(partial.at[2], 1)
    started += first + second

    low, high = masks

    def project(q, carry):
        rows = []
        for r in (2 * q, 2 * q + 1):
            b = blocks_of(stack, lidx_ref, r)
            at = [lidx_ref[r * K + k] // BLK for k in range(K)]
            lefts = []
            for o in range(3):
                c = [(at[k] == o).astype(F32) for k in range(K)]
                m = [(low.astype(F32) * c[k] if k % 2 == 0 else high.astype(F32) * c[k]).astype(BF16) for k in range(K)]
                lefts.append(
                    jnp.concatenate([b[0] * m[0] + b[1] * m[1], b[2] * m[2] + b[3] * m[3], b[4] * m[4]], axis=1)
                )
            out = dot(jnp.concatenate(lefts, axis=0), op_ref[r], NT)
            rows.append([fold(out[o * 2 * TS : (o + 1) * 2 * TS]) for o in range(3)])
        for o in range(3):
            x = jnp.where(low_lanes((TS, LANES)), rows[0][o], rows[1][o])
            mapped[o, :, columns(q)] = split(x)
        return carry

    lax.fori_loop(0, PAIRS, project, 0, unroll=2)
    h = [fold(dot(halves[...], mapped[o], NT)) for o in range(3)]
    is_first = (s == 0).astype(F32)
    is_last = (s == members - 1).astype(F32)
    term[0:HALF] = pack(is_first * h[0])
    term[HALF : 2 * HALF] = pack(h[1] + (1.0 - is_first) * h[0] + (1.0 - is_last) * h[2])
    term[2 * HALF : 3 * HALF] = pack(is_last * h[2])
    terms = [
        remote(term, final.at[s], term_send.at[i], term_recv.at[i], peer)
        for i, peer in enumerate(subs)
    ]
    for c in terms:
        c.start()
    final[s] = term[...]
    started += terms

    take(second)
    inverse2 = inverse_factor(sum_grp(1) / total_rows)
    wide2 = wide(inverse2)

    def finish(q, carry):
        basis_ref[:, columns(q)] = times(wide2, halves[:, columns(q)])
        return carry

    lax.fori_loop(0, PAIRS, finish, 0, unroll=4)

    take(terms)
    acc = final[0]
    for i in range(1, members):
        acc = acc + final[i]
    square = inverse2[:, :TS]
    for o in range(3):
        packed = acc[o * HALF : (o + 1) * HALF]
        h = jnp.concatenate([packed[:, :TS], roll(packed)[:, :TS]], axis=0)
        left = lax.dot_general(square, h, NN, precision=lax.Precision.HIGHEST, preferred_element_type=F32)
        full = lax.dot_general(left, square, NT, precision=lax.Precision.HIGHEST, preferred_element_type=F32)
        tail[:, o * LANES : o * LANES + TS] = full * (groups / total_rows)
    mine = pl.ds(pl.multiple_of(s * 8, 8), 8)
    for o in range(3):
        coarse_ref[:, o * TS : (o + 1) * TS] = tail[mine, o * LANES : o * LANES + TS]
    for c in started:
        c.wait_send()


def iterate(lidx, op, x1, g1, groups, members, total_rows):
    vmem = pl.BlockSpec(memory_space=pltpu.VMEM)
    dma = pltpu.SemaphoreType.DMA
    return pl.pallas_call(
        functools.partial(iterate_kernel, groups, members, total_rows),
        out_shape=(
            jax.ShapeDtypeStruct((TS, ROWS), F32),
            jax.ShapeDtypeStruct((TS // members, 3 * TS), F32),
        ),
        in_specs=[pl.BlockSpec(memory_space=pltpu.SMEM), vmem, vmem, vmem],
        out_specs=(vmem, vmem),
        scratch_shapes=[
            pltpu.VMEM((3 * BLK, 2 * TS, LANES), BF16),
            pltpu.VMEM((2, TS, ROWS), F32),
            pltpu.VMEM((2, TS, ROWS), F32),
            pltpu.VMEM((TS, ROWS), F32),
            pltpu.VMEM((2 * TS, ROWS), BF16),
            pltpu.VMEM((3, 2 * TS, ROWS), BF16),
            pltpu.VMEM((2, members, HALF, LANES), F32),
            pltpu.VMEM((2, groups, HALF, LANES), F32),
            pltpu.VMEM((3, HALF, LANES), F32),
            pltpu.VMEM((members, 3 * HALF, LANES), F32),
            pltpu.VMEM((3 * HALF, LANES), F32),
            pltpu.VMEM((TS, 3 * LANES), F32),
            dma((2, 2)),
            dma((2, 2)),
            dma((2, members - 1)),
            dma((2, members - 1)),
            dma((2, groups - 1)),
            dma((2, groups - 1)),
            dma((members - 1,)),
            dma((members - 1,)),
        ],
        compiler_params=pltpu.CompilerParams(
            collective_id=1, has_side_effects=True, vmem_limit_bytes=48 << 20
        ),
    )(lidx, op, x1, g1)


def shards(tiles, owner, slot, nbr, shift, start):
    axes = ("grp", "sub")
    groups, members = lax.axis_size("grp"), lax.axis_size("sub")
    devices = groups * members
    me = lax.axis_index(axes)
    count = tiles.shape[0]
    total_blocks = BLK * devices
    dest = owner[:, 0]

    order = jnp.arange(count, dtype=jnp.int32)
    earlier = (dest[:, None] == dest[None, :]) & (order[:, None] < order[None, :])
    rank = jnp.sum(earlier.astype(jnp.int32), axis=0)
    place = dest * CAP + rank
    x = tiles.transpose(1, 2, 0).reshape(2, HALF * TS, count)
    sent = route(place, x, devices * CAP).reshape(devices, CAP * HALF, LANES)
    got = lax.all_to_all(sent, axes, split_axis=0, concat_axis=0, tiled=True)

    codes = lax.all_gather(dest * (SLOTS + 1) + slot, axes, axis=0, tiled=False)
    mine = codes // (SLOTS + 1) == me
    target = codes % (SLOTS + 1)
    upto = (order[:, None] <= order[None, :]).astype(BF16)
    seen = dot(mine.astype(BF16), upto, NN)
    slots = jnp.stack(
        [
            jnp.sum(jnp.where(mine & (seen == k + 1.0), target - SLOTS, 0), axis=1) + SLOTS
            for k in range(CAP)
        ],
        axis=1,
    ).reshape(devices * CAP)

    own = start.T
    forward = [(i, (i + 1) % devices) for i in range(devices)]
    backward = [((i + 1) % devices, i) for i in range(devices)]
    left = lax.ppermute(own, axes, forward)
    right = lax.ppermute(own, axes, backward)
    lidx = ((nbr - (me - 1) * BLK) % total_blocks).reshape(SLOTS)
    twice = jnp.tile(shift.reshape(BLK, TS), (1, 2))
    op, x1, g1 = assemble(slots, lidx, got.reshape(devices * CAP * HALF, LANES), twice, left, own, right)
    basis, coarse = iterate(lidx, op, x1, g1, groups, members, float(total_blocks * TS))
    return basis.T, coarse[None]


def solution(mesh):
    placed = (
        P(("grp", "sub"), None, None),
        P(("grp", "sub"), None),
        P(("grp", "sub")),
        P(("grp", "sub"), None),
        P(("grp", "sub")),
        P(("grp", "sub"), None),
    )
    return jax.shard_map(
        shards,
        mesh=mesh,
        in_specs=placed,
        out_specs=(P(("grp", "sub"), None), P("grp", "sub", None)),
        check_vma=False,
    )
```

```python
import functools

import jax
import jax.numpy as jnp
from jax import lax
from jax.experimental import pallas as pl
from jax.experimental.pallas import tpu as pltpu
from jax.sharding import PartitionSpec as P

K = 5
CAP = 4
TS = 64
HALF = 32
LANES = 128
BLK = 32
ROWS = BLK * TS
PAIRS = ROWS // LANES
SLOTS = BLK * K
NT = (((1,), (1,)), ((), ()))
NN = (((1,), (0,)), ((), ()))
STRIDE = 37
SHIFT = 51
MESH = pl.DeviceIdType.MESH
F32 = jnp.float32
BF16 = jnp.bfloat16


def dot(a, b, dims):
    return lax.dot_general(a, b, dims, preferred_element_type=F32)


def roll(x):
    return pltpu.roll(x, TS, axis=1)


def low_lanes(shape):
    return lax.broadcasted_iota(jnp.int32, shape, 1) < TS


def split(x):
    hi = x.astype(BF16)
    lo = (x - hi.astype(F32)).astype(BF16)
    return jnp.concatenate([hi, lo], axis=0)


def fold(out):
    t = out[:TS] + out[TS:]
    return t + roll(t)


def spread(x):
    low = low_lanes(x.shape)
    r = roll(x)
    return jnp.where(low, x, r), jnp.where(low, r, x)


def pack(x):
    return jnp.where(low_lanes((HALF, LANES)), x[:HALF], x[HALF:])


def half_masks():
    low = low_lanes((1, LANES)).astype(F32)
    return low.astype(BF16), (1.0 - low).astype(BF16)


def blocks_of(stack_ref, lidx_ref, r):
    return [stack_ref[lidx_ref[r * K + k]] for k in range(K)]


def apply_row(stack_ref, lidx_ref, op_ref, r, masks):
    low, high = masks
    b = blocks_of(stack_ref, lidx_ref, r)
    left = jnp.concatenate([b[0] * low + b[1] * high, b[2] * low + b[3] * high, b[4]], axis=1)
    return fold(dot(left, op_ref[r], NT))


def inverse_factor(gram):
    lane = lax.broadcasted_iota(jnp.int32, (8, LANES), 1)
    row = lax.broadcasted_iota(jnp.int32, (8, LANES), 0)
    rolled = roll(gram)
    blocks = []
    for b in range(TS // 8):
        source = gram if b < 4 else rolled
        part = source[8 * (b % 4) : 8 * (b % 4) + 8]
        unit = (lane == row + (TS + 8 * b)).astype(F32)
        blocks.append(jnp.where(lane < TS, part, unit))
    for jb in range(TS // 8):
        cols = {
            b: [
                jnp.broadcast_to(blocks[b][:, 8 * jb + m : 8 * jb + m + 1], (8, LANES))
                for m in range(8)
            ]
            for b in range(jb, TS // 8)
        }
        e = [[jnp.broadcast_to(cols[jb][m][i : i + 1], (8, LANES)) for m in range(i + 1)] for i in range(8)]
        rows = [jnp.broadcast_to(blocks[jb][i : i + 1], (8, LANES)) for i in range(8)]
        l = [[None] * 8 for _ in range(8)]
        inv = []
        for m in range(8):
            inv.append(1.0 / e[m][m])
            for i in range(m + 1, 8):
                l[i][m] = e[i][m] * inv[m]
            for i in range(m + 1, 8):
                for k in range(m + 1, i + 1):
                    e[i][k] = e[i][k] - l[i][m] * e[k][m]
                rows[i] = rows[i] - l[i][m] * rows[m]
        solved = [None] * 8
        for m in reversed(range(8)):
            acc = rows[m] * inv[m]
            for i in reversed(range(m + 1, 8)):
                acc = acc - l[i][m] * solved[i]
            solved[m] = acc
        for b in range(jb + 1, TS // 8):
            acc = [cols[b][m] * solved[m] for m in range(8)]
            while len(acc) > 1:
                acc = [acc[i] + acc[i + 1] for i in range(0, len(acc), 2)]
            blocks[b] = blocks[b] - acc[0]
        done = rows[0] * lax.rsqrt(e[0][0])
        for m in range(1, 8):
            done = jnp.where(row == m, rows[m] * lax.rsqrt(e[m][m]), done)
        blocks[jb] = done
    a = jnp.concatenate(blocks, axis=0)
    return jnp.where(low_lanes(a.shape), roll(a), a)


def wide(inverse):
    hi = inverse.astype(BF16)
    lo = (inverse - hi.astype(F32)).astype(BF16)
    return jnp.concatenate([hi, lo], axis=1)


def times(inverse, x):
    return dot(inverse, jnp.concatenate([x, x], axis=0), NN)


def whole_kernel(
    groups, members, total_rows,
    index_ref, lidx_ref, info_ref, shift_ref, start_ref, x_ref,
    basis_ref, coarse_ref,
    tiles, packed, sent, got, info_got, total, op, x1,
    stack, halo0, halo1, halo2, z, halves, mapped, sub_got, grp_got, partial, final, term, tail,
    load_sem, tile_send, tile_recv, info_send, info_recv,
    halo_send, halo_recv, sub_send, sub_recv, grp_send, grp_recv, term_send, term_recv,
):
    g, s = lax.axis_index("grp"), lax.axis_index("sub")
    me = g * members + s
    count = groups * members
    after, before = lax.rem(me + 1, count), lax.rem(me + count - 1, count)

    def device(index):
        return (index // members, lax.rem(index, members))

    def peer_of(i):
        other = jnp.bitwise_xor(me, lax.rem(i * STRIDE + me * SHIFT, count - 1) + 1)
        return other, device(other)

    loads = [
        pltpu.make_async_copy(
            x_ref.at[:, :, pl.ds(h * LANES, LANES)], tiles.at[:, :, pl.ds(h * LANES, LANES)], load_sem.at[h]
        )
        for h in range(2)
    ]
    for c in loads:
        c.start()

    barrier = pltpu.get_barrier_semaphore()

    def greet(i, carry):
        pl.semaphore_signal(barrier, inc=1, device_id=peer_of(i)[1], device_id_type=MESH)
        return carry

    lax.fori_loop(0, count - 1, greet, 0)

    subs = [(g, lax.rem(s + i, members)) for i in range(1, members)]
    grps = [(lax.rem(g + i, groups), s) for i in range(1, groups)]

    for h in range(2):
        loads[h].wait()
        for c in range(HALF):
            block = jnp.concatenate(
                [
                    tiles[0, pl.ds(c * TS, TS), pl.ds(h * LANES, LANES)],
                    tiles[1, pl.ds(c * TS, TS), pl.ds(h * LANES, LANES)],
                ],
                axis=0,
            )
            packed[pl.ds(h * LANES, LANES), c, :] = block.T

    def tile(position):
        return packed[index_ref[position]]

    pl.semaphore_wait(barrier, count - 1)

    def remote(src, dst, send, recv, peer):
        return pltpu.make_async_remote_copy(
            src_ref=src, dst_ref=dst, send_sem=send, recv_sem=recv,
            device_id=peer, device_id_type=MESH,
        )

    def send_halo(src, halo, n):
        copies = [
            remote(src, halo.at[0], halo_send.at[n, 0], halo_recv.at[n, 0], device(after)),
            remote(src, halo.at[1], halo_send.at[n, 1], halo_recv.at[n, 1], device(before)),
        ]
        for c in copies:
            c.start()
        return copies

    def send_sub(src, got, sends, recvs, n):
        copies = [
            remote(src, got.at[n, s], sends.at[n, i], recvs.at[n, i], peer)
            for i, peer in enumerate(subs)
        ]
        for c in copies:
            c.start()
        return copies

    def send_grp(src, n):
        copies = [
            remote(src, grp_got.at[n, g], grp_send.at[n, i], grp_recv.at[n, i], peer)
            for i, peer in enumerate(grps)
        ]
        for c in copies:
            c.start()
        return copies

    def take(copies):
        for c in copies:
            c.wait_recv()

    def sum_sub(n):
        acc = sub_got[n, 0]
        for i in range(1, members):
            acc = acc + sub_got[n, i]
        return acc

    def sum_grp(n):
        acc = grp_got[n, 0]
        for i in range(1, groups):
            acc = acc + grp_got[n, i]
        return acc

    def columns(q):
        return pl.ds(pl.multiple_of(q * LANES, LANES), LANES)

    def put_pair(base, q, x):
        even, odd = spread(x)
        stack[base + 2 * q] = split(even)
        stack[base + 2 * q + 1] = split(odd)

    started = send_halo(start_ref, halo0, 0)
    halo = started[:]

    def info_copy(i):
        other, place = peer_of(i)
        return remote(info_ref.at[other], info_got.at[me], info_send, info_recv, place)

    def send_info(i, carry):
        info_copy(i).start()
        return carry

    def send_tiles(k):
        def send(i, carry):
            other, place = peer_of(i)
            sent[k, other] = tile(other * CAP + k)
            remote(sent.at[k, other], got.at[k, me], tile_send.at[k], tile_recv.at[k], place).start()
            return carry

        lax.fori_loop(0, count - 1, send, 0)

    send_tiles(0)
    lax.fori_loop(0, count - 1, send_info, 0)
    for k in range(1, CAP):
        send_tiles(k)
    for k in range(CAP):
        got[k, me] = tile(me * CAP + k)
    info_got[me] = info_ref[me]

    def own0(q, carry):
        put_pair(BLK, q, start_ref[:, columns(q)])
        return carry

    lax.fori_loop(0, PAIRS, own0, 0, unroll=2)
    take(halo)

    def spread_halo(ref, side, q, carry):
        put_pair(side * 2 * BLK, q, ref[side, :, columns(q)])
        return carry

    for side in range(2):
        lax.fori_loop(0, PAIRS, functools.partial(spread_halo, halo0, side), 0, unroll=2)

    def bulk(ref, send, recv):
        part = ref.at[pl.ds(0, count - 1)]
        return remote(part, part, send, recv, device(after))

    bulk(info_got, info_send, info_recv).wait_recv()
    slots = info_got[:, 0, :].T
    slot_iota = lax.broadcasted_iota(jnp.int32, (SLOTS, count), 0).astype(F32)
    for k in range(CAP):
        hot = (slot_iota == slots[k : k + 1]).astype(F32).astype(BF16)
        hot = jnp.concatenate([hot, hot], axis=1)
        bulk(got.at[k], tile_send.at[k], tile_recv.at[k]).wait_recv()

        def add(c, carry, k=k, hot=hot):
            new = dot(hot, split(got[k, :, c, :]), NN)
            total[c] = new if k == 0 else total[c] + new
            return carry

        lax.fori_loop(0, HALF, add, 0, unroll=2)

    low = low_lanes((HALF, LANES))
    row = lax.broadcasted_iota(jnp.int32, (HALF, LANES), 0)
    lane = lax.broadcasted_iota(jnp.int32, (HALF, LANES), 1)
    on_diagonal = (lane % TS) == row + HALF * (lane // TS)

    def form(r, carry):
        t = [total[:, r * K + k, :] for k in range(K)]
        t[0] = t[0] + jnp.where(on_diagonal, shift_ref[pl.ds(r, 1)], 0.0)
        for j in range(3):
            a = t[2 * j]
            b = t[2 * j + 1] if 2 * j + 1 < K else jnp.zeros_like(a)
            both = jnp.concatenate([jnp.where(low, a, roll(b)), jnp.where(low, roll(a), b)], axis=0)
            op[r, :, pl.ds(j * LANES, LANES)] = split(both)
        return carry

    lax.fori_loop(0, BLK, form, 0, unroll=2)

    masks = half_masks()

    def product(out, q, carry):
        even = apply_row(stack, lidx_ref, op, 2 * q, masks)
        odd = apply_row(stack, lidx_ref, op, 2 * q + 1, masks)
        out[:, columns(q)] = jnp.where(low_lanes(even.shape), even, odd)
        return carry

    lax.fori_loop(0, PAIRS, functools.partial(product, x1), 0, unroll=4)
    halo = send_halo(x1, halo1, 1)

    def own1(q, carry):
        x = x1[:, columns(q)]
        halves[:, columns(q)] = split(x)
        put_pair(BLK, q, x)
        return carry

    lax.fori_loop(0, PAIRS, own1, 0, unroll=2)
    partial[3] = pack(fold(dot(halves[...], halves[...], NT)))

    first = send_sub(partial.at[3], sub_got, sub_send, sub_recv, 0)
    sub_got[0, s] = partial[3]
    take(first)
    partial[0] = sum_sub(0)
    grp_got[0, g] = partial[0]
    second = send_grp(partial.at[0], 0)
    take(halo)
    started += first + halo + second

    for side in range(2):
        def ext1(q, carry, side=side):
            put_pair(side * 2 * BLK, q, halo1[side, :, columns(q)])
            return carry

        lax.fori_loop(0, PAIRS, ext1, 0, unroll=2)

    lax.fori_loop(0, PAIRS, functools.partial(product, z), 0, unroll=4)
    halo = send_halo(z, halo2, 2)
    started += halo

    take(second)
    inverse1 = wide(inverse_factor(sum_grp(0) / total_rows))

    def own2(q, carry):
        x = times(inverse1, split(z[:, columns(q)]))
        halves[:, columns(q)] = split(x)
        put_pair(BLK, q, x)
        return carry

    lax.fori_loop(0, PAIRS, own2, 0, unroll=4)
    partial[1] = pack(fold(dot(halves[...], halves[...], NT)))
    first = send_sub(partial.at[1], sub_got, sub_send, sub_recv, 1)
    sub_got[1, s] = partial[1]

    take(halo)
    for side in range(2):
        def ext2(q, carry, side=side):
            x = times(inverse1, split(halo2[side, :, columns(q)]))
            put_pair(side * 2 * BLK, q, x)
            return carry

        lax.fori_loop(0, PAIRS, ext2, 0, unroll=4)

    take(first)
    partial[2] = sum_sub(1)
    grp_got[1, g] = partial[2]
    second = send_grp(partial.at[2], 1)
    started += first + second

    low, high = masks

    def project(q, carry):
        rows = []
        for r in (2 * q, 2 * q + 1):
            b = blocks_of(stack, lidx_ref, r)
            at = [lidx_ref[r * K + k] // BLK for k in range(K)]
            lefts = []
            for o in range(3):
                c = [(at[k] == o).astype(F32) for k in range(K)]
                m = [(low.astype(F32) * c[k] if k % 2 == 0 else high.astype(F32) * c[k]).astype(BF16) for k in range(K)]
                lefts.append(
                    jnp.concatenate([b[0] * m[0] + b[1] * m[1], b[2] * m[2] + b[3] * m[3], b[4] * m[4]], axis=1)
                )
            out = dot(jnp.concatenate(lefts, axis=0), op[r], NT)
            rows.append([fold(out[o * 2 * TS : (o + 1) * 2 * TS]) for o in range(3)])
        for o in range(3):
            x = jnp.where(low_lanes((TS, LANES)), rows[0][o], rows[1][o])
            mapped[o, :, columns(q)] = split(x)
        return carry

    lax.fori_loop(0, PAIRS, project, 0, unroll=2)
    h = [fold(dot(halves[...], mapped[o], NT)) for o in range(3)]
    is_first = (s == 0).astype(F32)
    is_last = (s == members - 1).astype(F32)
    term[0:HALF] = pack(is_first * h[0])
    term[HALF : 2 * HALF] = pack(h[1] + (1.0 - is_first) * h[0] + (1.0 - is_last) * h[2])
    term[2 * HALF : 3 * HALF] = pack(is_last * h[2])
    terms = [
        remote(term, final.at[s], term_send.at[i], term_recv.at[i], peer)
        for i, peer in enumerate(subs)
    ]
    for c in terms:
        c.start()
    final[s] = term[...]
    started += terms

    take(second)
    inverse2 = inverse_factor(sum_grp(1) / total_rows)
    wide2 = wide(inverse2)

    def finish(q, carry):
        basis_ref[:, columns(q)] = times(wide2, halves[:, columns(q)])
        return carry

    lax.fori_loop(0, PAIRS, finish, 0, unroll=4)

    take(terms)
    acc = final[0]
    for i in range(1, members):
        acc = acc + final[i]
    square = inverse2[:, :TS]
    for o in range(3):
        packed = acc[o * HALF : (o + 1) * HALF]
        h = jnp.concatenate([packed[:, :TS], roll(packed)[:, :TS]], axis=0)
        left = lax.dot_general(square, h, NN, precision=lax.Precision.HIGHEST, preferred_element_type=F32)
        full = lax.dot_general(left, square, NT, precision=lax.Precision.HIGHEST, preferred_element_type=F32)
        tail[:, o * LANES : o * LANES + TS] = full * (groups / total_rows)
    mine = pl.ds(pl.multiple_of(s * 8, 8), 8)
    for o in range(3):
        coarse_ref[:, o * TS : (o + 1) * TS] = tail[mine, o * LANES : o * LANES + TS]
    for c in started:
        c.wait_send()
    for c in [bulk(info_got, info_send, info_recv)] + [
        bulk(sent.at[k], tile_send.at[k], tile_recv.at[k]) for k in range(CAP)
    ]:
        c.wait_send()


def whole(index, lidx, info, shift2, start, x, groups, members, total_rows):
    vmem, smem = pl.BlockSpec(memory_space=pltpu.VMEM), pl.BlockSpec(memory_space=pltpu.SMEM)
    dma = pltpu.SemaphoreType.DMA
    count = groups * members
    tiles = x.shape[2]
    return pl.pallas_call(
        functools.partial(whole_kernel, groups, members, total_rows),
        out_shape=(
            jax.ShapeDtypeStruct((TS, ROWS), F32),
            jax.ShapeDtypeStruct((TS // members, 3 * TS), F32),
        ),
        in_specs=[smem, smem, vmem, vmem, vmem, pl.BlockSpec(memory_space=pl.ANY)],
        out_specs=(vmem, vmem),
        scratch_shapes=[
            pltpu.VMEM((2, HALF * TS, tiles), F32),
            pltpu.VMEM((tiles, HALF, LANES), F32),
            pltpu.VMEM((CAP, count, HALF, LANES), F32),
            pltpu.VMEM((CAP, count, HALF, LANES), F32),
            pltpu.VMEM((count, 1, LANES), F32),
            pltpu.VMEM((HALF, SLOTS, LANES), F32),
            pltpu.VMEM((BLK, 2 * TS, 3 * LANES), BF16),
            pltpu.VMEM((TS, ROWS), F32),
            pltpu.VMEM((3 * BLK, 2 * TS, LANES), BF16),
            pltpu.VMEM((2, TS, ROWS), F32),
            pltpu.VMEM((2, TS, ROWS), F32),
            pltpu.VMEM((2, TS, ROWS), F32),
            pltpu.VMEM((TS, ROWS), F32),
            pltpu.VMEM((2 * TS, ROWS), BF16),
            pltpu.VMEM((3, 2 * TS, ROWS), BF16),
            pltpu.VMEM((2, members, HALF, LANES), F32),
            pltpu.VMEM((2, groups, HALF, LANES), F32),
            pltpu.VMEM((4, HALF, LANES), F32),
            pltpu.VMEM((members, 3 * HALF, LANES), F32),
            pltpu.VMEM((3 * HALF, LANES), F32),
            pltpu.VMEM((TS, 3 * LANES), F32),
            dma((2,)),
            dma((CAP,)),
            dma((CAP,)),
            dma,
            dma,
            dma((3, 2)),
            dma((3, 2)),
            dma((2, members - 1)),
            dma((2, members - 1)),
            dma((2, groups - 1)),
            dma((2, groups - 1)),
            dma((members - 1,)),
            dma((members - 1,)),
        ],
        compiler_params=pltpu.CompilerParams(
            collective_id=1, has_side_effects=True, vmem_limit_bytes=60 << 20
        ),
    )(index, lidx, info, shift2, start, x)


def shards(tiles, owner, slot, nbr, shift, start):
    axes = ("grp", "sub")
    groups, members = lax.axis_size("grp"), lax.axis_size("sub")
    devices = groups * members
    me = lax.axis_index(axes)
    count = tiles.shape[0]
    total_blocks = BLK * devices
    dest = owner[:, 0]

    order = jnp.arange(count, dtype=jnp.int32)
    earlier = (dest[:, None] == dest[None, :]) & (order[:, None] < order[None, :])
    rank = jnp.sum(earlier.astype(jnp.int32), axis=0)
    place = dest * CAP + rank
    hit = place[:, None] == jnp.arange(devices * CAP, dtype=jnp.int32)[None, :]
    index = jnp.sum(jnp.where(hit, order[:, None], 0), axis=0)
    named = jnp.sum(jnp.where(hit, slot[:, None] - SLOTS, 0), axis=0) + SLOTS
    info = jnp.pad(
        named.astype(F32).reshape(devices, 1, CAP),
        ((0, 0), (0, 0), (0, LANES - CAP)),
    )
    x = tiles.transpose(1, 2, 0).reshape(2, HALF * TS, count)
    lidx = ((nbr - (me - 1) * BLK) % total_blocks).reshape(SLOTS)
    twice = jnp.tile(shift.reshape(BLK, TS), (1, 2))
    basis, coarse = whole(
        index, lidx, info, twice, start.T, x, groups, members, float(total_blocks * TS)
    )
    return basis.T, coarse[None]


def solution(mesh):
    placed = (
        P(("grp", "sub"), None, None),
        P(("grp", "sub"), None),
        P(("grp", "sub")),
        P(("grp", "sub"), None),
        P(("grp", "sub")),
        P(("grp", "sub"), None),
    )
    return jax.shard_map(
        shards,
        mesh=mesh,
        in_specs=placed,
        out_specs=(P(("grp", "sub"), None), P("grp", "sub", None)),
        check_vma=False,
    )
```

```python
import functools

import jax
import jax.numpy as jnp
from jax import lax
from jax.experimental import pallas as pl
from jax.experimental.pallas import tpu as pltpu
from jax.sharding import PartitionSpec as P

K = 5
CAP = 4
TS = 64
HALF = 32
LANES = 128
BLK = 32
ROWS = BLK * TS
PAIRS = ROWS // LANES
SLOTS = BLK * K
NT = (((1,), (1,)), ((), ()))
NN = (((1,), (0,)), ((), ()))
PIECES = 4
STRIDE = 37
SHIFT = 51
MESH = pl.DeviceIdType.MESH
F32 = jnp.float32
BF16 = jnp.bfloat16


def dot(a, b, dims):
    return lax.dot_general(a, b, dims, preferred_element_type=F32)


def roll(x):
    return pltpu.roll(x, TS, axis=1)


def low_lanes(shape):
    return lax.broadcasted_iota(jnp.int32, shape, 1) < TS


def split(x):
    hi = x.astype(BF16)
    lo = (x - hi.astype(F32)).astype(BF16)
    return jnp.concatenate([hi, lo], axis=0)


def fold(out):
    t = out[:TS] + out[TS:]
    return t + roll(t)


def spread(x):
    low = low_lanes(x.shape)
    r = roll(x)
    return jnp.where(low, x, r), jnp.where(low, r, x)


def pack(x):
    return jnp.where(low_lanes((HALF, LANES)), x[:HALF], x[HALF:])


def half_masks():
    low = low_lanes((1, LANES)).astype(F32)
    return low.astype(BF16), (1.0 - low).astype(BF16)


def blocks_of(stack_ref, lidx_ref, r):
    return [stack_ref[jnp.clip(lidx_ref[k, r], 0, 3 * BLK - 1)] for k in range(K)]


def apply_row(stack_ref, lidx_ref, op_ref, r, masks):
    low, high = masks
    b = blocks_of(stack_ref, lidx_ref, r)
    left = jnp.concatenate([b[0] * low + b[1] * high, b[2] * low + b[3] * high, b[4]], axis=1)
    return fold(dot(left, op_ref[r], NT))


def inverse_factor(gram):
    lane = lax.broadcasted_iota(jnp.int32, (8, LANES), 1)
    row = lax.broadcasted_iota(jnp.int32, (8, LANES), 0)
    rolled = roll(gram)
    blocks = []
    for b in range(TS // 8):
        source = gram if b < 4 else rolled
        part = source[8 * (b % 4) : 8 * (b % 4) + 8]
        unit = (lane == row + (TS + 8 * b)).astype(F32)
        blocks.append(jnp.where(lane < TS, part, unit))
    for jb in range(TS // 8):
        cols = {
            b: [
                jnp.broadcast_to(blocks[b][:, 8 * jb + m : 8 * jb + m + 1], (8, LANES))
                for m in range(8)
            ]
            for b in range(jb, TS // 8)
        }
        e = [[jnp.broadcast_to(cols[jb][m][i : i + 1], (8, LANES)) for m in range(i + 1)] for i in range(8)]
        rows = [jnp.broadcast_to(blocks[jb][i : i + 1], (8, LANES)) for i in range(8)]
        l = [[None] * 8 for _ in range(8)]
        inv = []
        for m in range(8):
            inv.append(1.0 / e[m][m])
            for i in range(m + 1, 8):
                l[i][m] = e[i][m] * inv[m]
            for i in range(m + 1, 8):
                for k in range(m + 1, i + 1):
                    e[i][k] = e[i][k] - l[i][m] * e[k][m]
                rows[i] = rows[i] - l[i][m] * rows[m]
        solved = [None] * 8
        for m in reversed(range(8)):
            acc = rows[m] * inv[m]
            for i in reversed(range(m + 1, 8)):
                acc = acc - l[i][m] * solved[i]
            solved[m] = acc
        for b in range(jb + 1, TS // 8):
            acc = [cols[b][m] * solved[m] for m in range(8)]
            while len(acc) > 1:
                acc = [acc[i] + acc[i + 1] for i in range(0, len(acc), 2)]
            blocks[b] = blocks[b] - acc[0]
        done = rows[0] * lax.rsqrt(e[0][0])
        for m in range(1, 8):
            done = jnp.where(row == m, rows[m] * lax.rsqrt(e[m][m]), done)
        blocks[jb] = done
    a = jnp.concatenate(blocks, axis=0)
    return jnp.where(low_lanes(a.shape), roll(a), a)


def wide(inverse):
    hi = inverse.astype(BF16)
    lo = (inverse - hi.astype(F32)).astype(BF16)
    return jnp.concatenate([hi, lo], axis=1)


def times(inverse, x):
    return dot(inverse, jnp.concatenate([x, x], axis=0), NN)


def whole_kernel(
    groups, members, total_rows,
    owner_ref, slot_ref, nbr_ref, shift_ref, start_ref, x_ref,
    halves, inverse_ref, acc_ref,
    index_v, index_ref, lidx_v, lidx_ref, info_ref, tiles, packed, sent, got, info_got, total, op, x1,
    stack, halo0, halo1, halo2, z, mapped, sub_got, grp_got, partial, final, term,
    load_sem, table_sem, tile_send, tile_recv, info_send, info_recv,
    halo_send, halo_recv, sub_send, sub_recv, grp_send, grp_recv, term_send, term_recv,
):
    g, s = lax.axis_index("grp"), lax.axis_index("sub")
    me = g * members + s
    count = groups * members
    after, before = lax.rem(me + 1, count), lax.rem(me + count - 1, count)

    def device(index):
        return (index // members, lax.rem(index, members))

    def peer_of(i):
        other = jnp.bitwise_xor(me, lax.rem(i * STRIDE + me * SHIFT, count - 1) + 1)
        return other, device(other)

    loads = [
        pltpu.make_async_copy(
            x_ref.at[:, :, pl.ds(h * LANES, LANES)], tiles.at[:, :, pl.ds(h * LANES, LANES)], load_sem.at[h]
        )
        for h in range(2)
    ]
    for c in loads:
        c.start()

    barrier = pltpu.get_barrier_semaphore()

    def greet(i, carry):
        pl.semaphore_signal(barrier, inc=1, device_id=peer_of(i)[1], device_id_type=MESH)
        return carry

    lax.fori_loop(0, count - 1, greet, 0)

    amount = owner_ref.shape[1]
    places = CAP * count

    def column(x, width):
        tall = jnp.broadcast_to(x, (8, x.shape[1])).T
        return jnp.broadcast_to(tall[:, :1], (x.shape[1], width))

    dest = owner_ref[...].astype(F32)
    down = lax.broadcasted_iota(jnp.int32, (amount, amount), 0)
    across = lax.broadcasted_iota(jnp.int32, (amount, amount), 1)
    earlier = (column(dest, amount) == dest) & (down < across)
    rank = jnp.sum(jnp.where(earlier, 1.0, 0.0), axis=0, keepdims=True)
    place = column(rank * count + dest, places)
    hit = place == lax.broadcasted_iota(jnp.int32, (amount, places), 1).astype(F32)
    order = lax.broadcasted_iota(jnp.int32, (amount, places), 0).astype(F32)
    index_v[...] = jnp.sum(jnp.where(hit, order, 0.0), axis=0, keepdims=True).astype(jnp.int32)
    target = column(slot_ref[...].astype(F32) - SLOTS, places)
    named = jnp.sum(jnp.where(hit, target, 0.0), axis=0, keepdims=True) + SLOTS
    info = jnp.concatenate(
        [named[:, k * count : (k + 1) * count] for k in range(CAP)] + [jnp.zeros((8 - CAP, count), F32)],
        axis=0,
    )
    info_ref[:, 0, :] = jnp.concatenate([info.T, jnp.zeros((count, LANES - 8), F32)], axis=1)
    near = nbr_ref[...] - (me - 1) * BLK
    near = jnp.where(near < 0, near + BLK * count, near)
    near = jnp.where(near >= BLK * count, near - BLK * count, near)
    lidx_v[0:K, 0:BLK] = jnp.minimum(near, 3 * BLK - 1)
    tables = [
        pltpu.make_async_copy(index_v, index_ref, table_sem.at[0]),
        pltpu.make_async_copy(lidx_v, lidx_ref, table_sem.at[1]),
    ]
    for c in tables:
        c.start()

    subs = [(g, lax.rem(s + i, members)) for i in range(1, members)]
    grps = [(lax.rem(g + i, groups), s) for i in range(1, groups)]

    for h in range(2):
        loads[h].wait()
        for c in range(HALF):
            block = jnp.concatenate(
                [
                    tiles[0, pl.ds(c * TS, TS), pl.ds(h * LANES, LANES)],
                    tiles[1, pl.ds(c * TS, TS), pl.ds(h * LANES, LANES)],
                ],
                axis=0,
            )
            packed[pl.ds(h * LANES, LANES), c, :] = block.T

    def tile(position):
        return packed[jnp.clip(index_ref[0, position], 0, amount - 1)]

    for c in tables:
        c.wait()
    pl.semaphore_wait(barrier, count - 1)

    def remote(src, dst, send, recv, peer):
        return pltpu.make_async_remote_copy(
            src_ref=src, dst_ref=dst, send_sem=send, recv_sem=recv,
            device_id=peer, device_id_type=MESH,
        )

    def piece(p):
        return pl.ds(p * (ROWS // PIECES), ROWS // PIECES)

    def send_halo(src, halo, n, p):
        copies = [
            remote(
                src.at[:, piece(p)], halo.at[0, :, piece(p)],
                halo_send.at[n, 0, p], halo_recv.at[n, 0, p], device(after),
            ),
            remote(
                src.at[:, piece(p)], halo.at[1, :, piece(p)],
                halo_send.at[n, 1, p], halo_recv.at[n, 1, p], device(before),
            ),
        ]
        for c in copies:
            c.start()
        return copies

    def send_sub(src, got, sends, recvs, n):
        copies = [
            remote(src, got.at[n, s], sends.at[n, i], recvs.at[n, i], peer)
            for i, peer in enumerate(subs)
        ]
        for c in copies:
            c.start()
        return copies

    def send_grp(src, n):
        copies = [
            remote(src, grp_got.at[n, g], grp_send.at[n, i], grp_recv.at[n, i], peer)
            for i, peer in enumerate(grps)
        ]
        for c in copies:
            c.start()
        return copies

    def take(copies):
        for c in copies:
            c.wait_recv()

    def sum_sub(n):
        acc = sub_got[n, 0]
        for i in range(1, members):
            acc = acc + sub_got[n, i]
        return acc

    def sum_grp(n):
        acc = grp_got[n, 0]
        for i in range(1, groups):
            acc = acc + grp_got[n, i]
        return acc

    def columns(q):
        return pl.ds(pl.multiple_of(q * LANES, LANES), LANES)

    def put_pair(base, q, x):
        even, odd = spread(x)
        stack[base + 2 * q] = split(even)
        stack[base + 2 * q + 1] = split(odd)


    def info_copy(i):
        other, place = peer_of(i)
        return remote(info_ref.at[other], info_got.at[me], info_send, info_recv, place)

    def send_info(i, carry):
        info_copy(i).start()
        return carry

    def send_tile(k, i):
        other, place = peer_of(i)
        sent[k, other] = tile(k * count + other)
        remote(sent.at[k, other], got.at[k, me], tile_send.at[k], tile_recv.at[k], place).start()

    def send_tiles(k):
        def send(i, carry):
            send_tile(k, i)
            return carry

        lax.fori_loop(0, count - 1, send, 0)

    def bulk(ref, send, recv):
        part = ref.at[pl.ds(0, count - 1)]
        return remote(part, part, send, recv, device(after))

    def arrived(k):
        bulk(got.at[k], tile_send.at[k], tile_recv.at[k]).wait_recv()

    for k in range(CAP):
        got[k, me] = tile(k * count + me)
    info_got[me] = info_ref[me]
    send_tiles(0)
    lax.fori_loop(0, count - 1, send_info, 0)
    send_tiles(1)

    def own0(q, carry):
        put_pair(BLK, q, start_ref[:, columns(q)])
        return carry

    lax.fori_loop(0, PAIRS, own0, 0, unroll=2)

    bulk(info_got, info_send, info_recv).wait_recv()
    slots = info_got[:, 0, :].T
    slot_iota = lax.broadcasted_iota(jnp.int32, (SLOTS, count), 0).astype(F32)

    def hot_of(k):
        hot = (slot_iota == slots[k : k + 1]).astype(F32).astype(BF16)
        return jnp.concatenate([hot, hot], axis=1)

    def add(k, hot, c):
        new = dot(hot, split(got[k, :, c, :]), NN)
        total[c] = new if k == 0 else total[c] + new

    for k in range(2, CAP):
        arrived(k - 2)
        hot = hot_of(k - 2)

        def both(c, carry, k=k, hot=hot):
            for j in range(count // HALF):
                i = c * (count // HALF) + j
                if j < count // HALF - 1:
                    send_tile(k, i)
                else:
                    @pl.when(i < count - 1)
                    def _():
                        send_tile(k, i)
            add(k - 2, hot, c)
            return carry

        lax.fori_loop(0, HALF, both, 0)

    halo = [send_halo(start_ref, halo0, 0, p) for p in range(PIECES)]
    started = sum(halo, [])
    for k in range(CAP - 2, CAP):
        arrived(k)
        hot = hot_of(k)

        def one(c, carry, k=k, hot=hot):
            add(k, hot, c)
            return carry

        lax.fori_loop(0, HALF, one, 0, unroll=8)

    low = low_lanes((HALF, LANES))
    row = lax.broadcasted_iota(jnp.int32, (HALF, LANES), 0)
    lane = lax.broadcasted_iota(jnp.int32, (HALF, LANES), 1)
    on_diagonal = (lane % TS) == row + HALF * (lane // TS)

    def form(q, carry):
        both = shift_ref[pl.ds(q, 1)]
        shift_of = [jnp.where(low[:1], both, roll(both)), jnp.where(low[:1], roll(both), both)]
        for b in range(2):
            r = 2 * q + b
            t = [total[:, r * K + k, :] for k in range(K)]
            t[0] = t[0] + jnp.where(on_diagonal, shift_of[b], 0.0)
            for j in range(3):
                x = t[2 * j]
                y = t[2 * j + 1] if 2 * j + 1 < K else jnp.zeros_like(x)
                pair = jnp.concatenate([jnp.where(low, x, roll(y)), jnp.where(low, roll(x), y)], axis=0)
                op[r, :, pl.ds(j * LANES, LANES)] = split(pair)
        return carry

    lax.fori_loop(0, PAIRS, form, 0, unroll=2)

    def spread_halo(ref, side, q, carry):
        put_pair(side * 2 * BLK, q, ref[side, :, columns(q)])
        return carry

    def spread_halos(ref, halo):
        for p in range(PIECES):
            take(halo[p])
            for side in range(2):
                lax.fori_loop(
                    p * (PAIRS // PIECES), (p + 1) * (PAIRS // PIECES),
                    functools.partial(spread_halo, ref, side), 0, unroll=4,
                )

    spread_halos(halo0, halo)

    masks = half_masks()

    def product(out, q, carry):
        even = apply_row(stack, lidx_ref, op, 2 * q, masks)
        odd = apply_row(stack, lidx_ref, op, 2 * q + 1, masks)
        out[:, columns(q)] = jnp.where(low_lanes(even.shape), even, odd)
        return carry

    def products(out, halo, n):
        copies = []
        for p in range(PIECES):
            lax.fori_loop(
                p * (PAIRS // PIECES), (p + 1) * (PAIRS // PIECES),
                functools.partial(product, out), 0, unroll=4,
            )
            copies.append(send_halo(out, halo, n, p))
        return copies

    halo = products(x1, halo1, 1)
    started += sum(halo, [])

    def own1(q, carry):
        x = x1[:, columns(q)]
        halves[:, columns(q)] = split(x)
        put_pair(BLK, q, x)
        return carry

    lax.fori_loop(0, PAIRS, own1, 0, unroll=2)
    partial[3] = pack(fold(dot(halves[...], halves[...], NT)))

    first = send_sub(partial.at[3], sub_got, sub_send, sub_recv, 0)
    sub_got[0, s] = partial[3]
    take(first)
    partial[0] = sum_sub(0)
    grp_got[0, g] = partial[0]
    second = send_grp(partial.at[0], 0)
    started += first + second
    spread_halos(halo1, halo)
    halo = products(z, halo2, 2)
    started += sum(halo, [])

    take(second)
    inverse1 = wide(inverse_factor(sum_grp(0) / total_rows))

    def own2(q, carry):
        x = times(inverse1, split(z[:, columns(q)]))
        halves[:, columns(q)] = split(x)
        put_pair(BLK, q, x)
        return carry

    lax.fori_loop(0, PAIRS, own2, 0, unroll=4)
    partial[1] = pack(fold(dot(halves[...], halves[...], NT)))
    first = send_sub(partial.at[1], sub_got, sub_send, sub_recv, 1)
    sub_got[1, s] = partial[1]

    def ext2(side, q, carry):
        put_pair(side * 2 * BLK, q, times(inverse1, split(halo2[side, :, columns(q)])))
        return carry

    for p in range(PIECES):
        take(halo[p])
        for side in range(2):
            lax.fori_loop(
                p * (PAIRS // PIECES), (p + 1) * (PAIRS // PIECES),
                functools.partial(ext2, side), 0, unroll=4,
            )

    take(first)
    partial[2] = sum_sub(1)
    grp_got[1, g] = partial[2]
    second = send_grp(partial.at[2], 1)
    started += first + second

    low, high = masks

    def project(q, carry):
        rows = []
        for r in (2 * q, 2 * q + 1):
            b = blocks_of(stack, lidx_ref, r)
            at = [lidx_ref[k, r] // BLK for k in range(K)]
            lefts = []
            for o in range(3):
                c = [(at[k] == o).astype(F32) for k in range(K)]
                m = [(low.astype(F32) * c[k] if k % 2 == 0 else high.astype(F32) * c[k]).astype(BF16) for k in range(K)]
                lefts.append(
                    jnp.concatenate([b[0] * m[0] + b[1] * m[1], b[2] * m[2] + b[3] * m[3], b[4] * m[4]], axis=1)
                )
            out = dot(jnp.concatenate(lefts, axis=0), op[r], NT)
            rows.append([fold(out[o * 2 * TS : (o + 1) * 2 * TS]) for o in range(3)])
        for o in range(3):
            x = jnp.where(low_lanes((TS, LANES)), rows[0][o], rows[1][o])
            mapped[o, :, columns(q)] = split(x)
        return carry

    lax.fori_loop(0, PAIRS, project, 0, unroll=2)
    h = [fold(dot(halves[...], mapped[o], NT)) for o in range(3)]
    is_first = (s == 0).astype(F32)
    is_last = (s == members - 1).astype(F32)
    term[0:HALF] = pack(is_first * h[0])
    term[HALF : 2 * HALF] = pack(h[1] + (1.0 - is_first) * h[0] + (1.0 - is_last) * h[2])
    term[2 * HALF : 3 * HALF] = pack(is_last * h[2])
    terms = [
        remote(term, final.at[s], term_send.at[i], term_recv.at[i], peer)
        for i, peer in enumerate(subs)
    ]
    for c in terms:
        c.start()
    final[s] = term[...]
    started += terms

    take(second)
    inverse_ref[...] = inverse_factor(sum_grp(1) / total_rows)
    take(terms)
    acc = final[0]
    for i in range(1, members):
        acc = acc + final[i]
    acc_ref[...] = acc
    for c in started:
        c.wait_send()
    for c in [bulk(info_got, info_send, info_recv)] + [
        bulk(sent.at[k], tile_send.at[k], tile_recv.at[k]) for k in range(CAP)
    ]:
        c.wait_send()


def whole(owner, slot, nbr, shift, start, x, groups, members, total_rows):
    vmem = pl.BlockSpec(memory_space=pltpu.VMEM)
    dma = pltpu.SemaphoreType.DMA
    count = groups * members
    tiles = x.shape[2]
    return pl.pallas_call(
        functools.partial(whole_kernel, groups, members, total_rows),
        out_shape=(
            jax.ShapeDtypeStruct((2 * TS, ROWS), BF16),
            jax.ShapeDtypeStruct((TS, LANES), F32),
            jax.ShapeDtypeStruct((3 * HALF, LANES), F32),
        ),
        in_specs=[vmem, vmem, vmem, vmem, vmem, pl.BlockSpec(memory_space=pl.ANY)],
        out_specs=(vmem, vmem, vmem),
        scratch_shapes=[
            pltpu.VMEM((1, CAP * count), jnp.int32),
            pltpu.SMEM((1, CAP * count), jnp.int32),
            pltpu.VMEM((8, LANES), jnp.int32),
            pltpu.SMEM((8, LANES), jnp.int32),
            pltpu.VMEM((count, 1, LANES), F32),
            pltpu.VMEM((2, HALF * TS, tiles), F32),
            pltpu.VMEM((tiles, HALF, LANES), F32),
            pltpu.VMEM((CAP, count, HALF, LANES), F32),
            pltpu.VMEM((CAP, count, HALF, LANES), F32),
            pltpu.VMEM((count, 1, LANES), F32),
            pltpu.VMEM((HALF, SLOTS, LANES), F32),
            pltpu.VMEM((BLK, 2 * TS, 3 * LANES), BF16),
            pltpu.VMEM((TS, ROWS), F32),
            pltpu.VMEM((3 * BLK, 2 * TS, LANES), BF16),
            pltpu.VMEM((2, TS, ROWS), F32),
            pltpu.VMEM((2, TS, ROWS), F32),
            pltpu.VMEM((2, TS, ROWS), F32),
            pltpu.VMEM((TS, ROWS), F32),
            pltpu.VMEM((3, 2 * TS, ROWS), BF16),
            pltpu.VMEM((2, members, HALF, LANES), F32),
            pltpu.VMEM((2, groups, HALF, LANES), F32),
            pltpu.VMEM((4, HALF, LANES), F32),
            pltpu.VMEM((members, 3 * HALF, LANES), F32),
            pltpu.VMEM((3 * HALF, LANES), F32),
            dma((2,)),
            dma((2,)),
            dma((CAP,)),
            dma((CAP,)),
            dma,
            dma,
            dma((3, 2, PIECES)),
            dma((3, 2, PIECES)),
            dma((2, members - 1)),
            dma((2, members - 1)),
            dma((2, groups - 1)),
            dma((2, groups - 1)),
            dma((members - 1,)),
            dma((members - 1,)),
        ],
        compiler_params=pltpu.CompilerParams(
            collective_id=1, has_side_effects=True, vmem_limit_bytes=60 << 20
        ),
    )(owner, slot, nbr, shift, start, x)


def finish_kernel(groups, members, total_rows, halves_ref, inverse_ref, acc_ref, basis_ref, coarse_ref, tail):
    inverse = inverse_ref[...]
    step = pl.program_id(0)
    basis_ref[...] = times(wide(inverse), halves_ref[...])

    @pl.when(step == 0)
    def _():
        square = inverse[:, :TS]
        for o in range(3):
            packed = acc_ref[o * HALF : (o + 1) * HALF]
            h = jnp.concatenate([packed[:, :TS], roll(packed)[:, :TS]], axis=0)
            left = lax.dot_general(
                square, h, NN, precision=lax.Precision.HIGHEST, preferred_element_type=F32
            )
            full = lax.dot_general(
                left, square, NT, precision=lax.Precision.HIGHEST, preferred_element_type=F32
            )
            tail[:, o * LANES : o * LANES + TS] = full * (groups / total_rows)
        each = TS // members
        mine = pl.ds(pl.multiple_of(lax.axis_index("sub") * each, each), each)
        for o in range(3):
            coarse_ref[:, o * TS : (o + 1) * TS] = tail[mine, o * LANES : o * LANES + TS]


def finish(halves, inverse, acc, groups, members, total_rows):
    steps = 4
    return pl.pallas_call(
        functools.partial(finish_kernel, groups, members, total_rows),
        out_shape=(
            jax.ShapeDtypeStruct((TS, ROWS), F32),
            jax.ShapeDtypeStruct((TS // members, 3 * TS), F32),
        ),
        grid=(steps,),
        in_specs=[
            pl.BlockSpec((2 * TS, ROWS // steps), lambda i: (0, i)),
            pl.BlockSpec((TS, LANES), lambda i: (0, 0)),
            pl.BlockSpec((3 * HALF, LANES), lambda i: (0, 0)),
        ],
        out_specs=(
            pl.BlockSpec((TS, ROWS // steps), lambda i: (0, i)),
            pl.BlockSpec((TS // members, 3 * TS), lambda i: (0, 0)),
        ),
        scratch_shapes=[pltpu.VMEM((TS, 3 * LANES), F32)],
    )(halves, inverse, acc)


def shards(tiles, owner, slot, nbr, shift, start):
    groups, members = lax.axis_size("grp"), lax.axis_size("sub")
    total_rows = float(ROWS * groups * members)
    count = tiles.shape[0]
    x = tiles.transpose(1, 2, 0).reshape(2, HALF * TS, count)
    halves, inverse, acc = whole(
        owner.T, slot.reshape(1, count), nbr.T, shift.reshape(PAIRS, LANES), start.T, x,
        groups, members, total_rows,
    )
    basis, coarse = finish(halves, inverse, acc, groups, members, total_rows)
    return basis.T, coarse[None]


def solution(mesh):
    placed = (
        P(("grp", "sub"), None, None),
        P(("grp", "sub"), None),
        P(("grp", "sub")),
        P(("grp", "sub"), None),
        P(("grp", "sub")),
        P(("grp", "sub"), None),
    )
    return jax.shard_map(
        shards,
        mesh=mesh,
        in_specs=placed,
        out_specs=(P(("grp", "sub"), None), P("grp", "sub", None)),
        check_vma=False,
    )
```

```python
import functools

import jax
import jax.numpy as jnp
from jax import lax
from jax.experimental import pallas as pl
from jax.experimental.pallas import tpu as pltpu
from jax.sharding import PartitionSpec as P

K = 5
CAP = 4
TS = 64
HALF = 32
PITCH = 40
LANES = 128
BLK = 32
ROWS = BLK * TS
PAIRS = ROWS // LANES
SLOTS = BLK * K
DEPTH = SLOTS + 8
NT = (((1,), (1,)), ((), ()))
NN = (((1,), (0,)), ((), ()))
PIECES = 4
STRIDE = 37
SHIFT = 51
MESH = pl.DeviceIdType.MESH
F32 = jnp.float32
BF16 = jnp.bfloat16


def dot(a, b, dims):
    return lax.dot_general(a, b, dims, preferred_element_type=F32)


def exact(a, b, dims):
    return lax.dot_general(a, b, dims, precision=lax.Precision.HIGHEST, preferred_element_type=F32)


def roll(x):
    return pltpu.roll(x, TS, axis=1)


def low_lanes(shape):
    return lax.broadcasted_iota(jnp.int32, shape, 1) < TS


def split(x):
    hi = x.astype(BF16)
    lo = (x - hi.astype(F32)).astype(BF16)
    return jnp.concatenate([hi, lo], axis=0)


def fold(out):
    t = out[:TS] + out[TS:]
    return t + roll(t)


def gram_parts(x):
    hi = x.astype(BF16)
    rest = x - hi.astype(F32)
    mid = rest.astype(BF16)
    lo = (rest - mid.astype(F32)).astype(BF16)
    return jnp.concatenate([hi, mid, lo, jnp.zeros_like(lo)], axis=0)


def fold_gram(out):
    t = out[:TS] + out[TS : 2 * TS] + out[2 * TS : 3 * TS]
    t = t[:, :LANES] + t[:, LANES:]
    return t + roll(t)


def spread(x):
    low = low_lanes(x.shape)
    r = roll(x)
    return jnp.where(low, x, r), jnp.where(low, r, x)


def pack(x):
    return jnp.where(low_lanes((HALF, LANES)), x[:HALF], x[HALF:])


def half_masks():
    low = low_lanes((1, LANES)).astype(F32)
    return low.astype(BF16), (1.0 - low).astype(BF16)


def blocks_of(stack_ref, lidx_ref, r):
    return [stack_ref[jnp.clip(lidx_ref[k, r], 0, 3 * BLK - 1)] for k in range(K)]


def apply_row(stack_ref, lidx_ref, op_ref, r, masks):
    low, high = masks
    b = blocks_of(stack_ref, lidx_ref, r)
    left = jnp.concatenate([b[0] * low + b[1] * high, b[2] * low + b[3] * high, b[4]], axis=1)
    return fold(dot(left, op_ref[r], NT))


def inverse_factor(gram):
    lane = lax.broadcasted_iota(jnp.int32, (8, LANES), 1)
    row = lax.broadcasted_iota(jnp.int32, (8, LANES), 0)
    rolled = roll(gram)
    blocks = []
    for b in range(TS // 8):
        source = gram if b < 4 else rolled
        part = source[8 * (b % 4) : 8 * (b % 4) + 8]
        unit = (lane == row + (TS + 8 * b)).astype(F32)
        blocks.append(jnp.where(lane < TS, part, unit))
    for jb in range(TS // 8):
        cols = {
            b: [
                jnp.broadcast_to(blocks[b][:, 8 * jb + m : 8 * jb + m + 1], (8, LANES))
                for m in range(8)
            ]
            for b in range(jb, TS // 8)
        }
        e = [[jnp.broadcast_to(cols[jb][m][i : i + 1], (8, LANES)) for m in range(i + 1)] for i in range(8)]
        rows = [jnp.broadcast_to(blocks[jb][i : i + 1], (8, LANES)) for i in range(8)]
        l = [[None] * 8 for _ in range(8)]
        inv = []
        for m in range(8):
            inv.append(1.0 / e[m][m])
            for i in range(m + 1, 8):
                l[i][m] = e[i][m] * inv[m]
            for i in range(m + 1, 8):
                for k in range(m + 1, i + 1):
                    e[i][k] = e[i][k] - l[i][m] * e[k][m]
                rows[i] = rows[i] - l[i][m] * rows[m]
        solved = [None] * 8
        for m in reversed(range(8)):
            acc = rows[m] * inv[m]
            for i in reversed(range(m + 1, 8)):
                acc = acc - l[i][m] * solved[i]
            solved[m] = acc
        for b in range(jb + 1, TS // 8):
            acc = [cols[b][m] * solved[m] for m in range(8)]
            while len(acc) > 1:
                acc = [acc[i] + acc[i + 1] for i in range(0, len(acc), 2)]
            blocks[b] = blocks[b] - acc[0]
        done = rows[0] * lax.rsqrt(e[0][0])
        for m in range(1, 8):
            done = jnp.where(row == m, rows[m] * lax.rsqrt(e[m][m]), done)
        blocks[jb] = done
    a = jnp.concatenate(blocks, axis=0)
    return jnp.where(low_lanes(a.shape), roll(a), a)


def wide(inverse):
    hi = inverse.astype(BF16)
    lo = (inverse - hi.astype(F32)).astype(BF16)
    return jnp.concatenate([hi, lo], axis=1)


def times(inverse, x):
    return dot(inverse, jnp.concatenate([x, x], axis=0), NN)


def whole_kernel(
    groups, members, total_rows,
    owner_ref, slot_ref, nbr_ref, shift_ref, start_ref, x_ref,
    halves, inverse_ref, acc_ref,
    index_v, index_ref, lidx_v, lidx_ref, info_ref, tiles, packed, sent, got, info_got, total, op, x1,
    stack, halo0, halo1, halo2, z, mapped, sub_got, grp_got, partial, final, term,
    load_sem, table_sem, tile_send, tile_recv, info_send, info_recv,
    halo_send, halo_recv, sub_send, sub_recv, grp_send, grp_recv, term_send, term_recv,
):
    g, s = lax.axis_index("grp"), lax.axis_index("sub")
    me = g * members + s
    count = groups * members
    after, before = lax.rem(me + 1, count), lax.rem(me + count - 1, count)

    def device(index):
        return (index // members, lax.rem(index, members))

    def peer_of(i):
        other = jnp.bitwise_xor(me, lax.rem(i * STRIDE + me * SHIFT, count - 1) + 1)
        return other, device(other)

    loads = [
        pltpu.make_async_copy(
            x_ref.at[:, :, pl.ds(h * LANES, LANES)], tiles.at[:, :, pl.ds(h * LANES, LANES)], load_sem.at[h]
        )
        for h in range(2)
    ]
    for c in loads:
        c.start()

    barrier = pltpu.get_barrier_semaphore()

    def greet(i, carry):
        pl.semaphore_signal(barrier, inc=1, device_id=peer_of(i)[1], device_id_type=MESH)
        return carry

    lax.fori_loop(0, count - 1, greet, 0)

    amount = owner_ref.shape[1]
    places = CAP * count

    def column(x, width):
        tall = jnp.broadcast_to(x, (8, x.shape[1])).T
        return jnp.broadcast_to(tall[:, :1], (x.shape[1], width))

    dest = owner_ref[...].astype(F32)
    down = lax.broadcasted_iota(jnp.int32, (amount, amount), 0)
    across = lax.broadcasted_iota(jnp.int32, (amount, amount), 1)
    earlier = (column(dest, amount) == dest) & (down < across)
    rank = jnp.sum(jnp.where(earlier, 1.0, 0.0), axis=0, keepdims=True)
    place = column(rank * count + dest, places)
    hit = place == lax.broadcasted_iota(jnp.int32, (amount, places), 1).astype(F32)
    order = lax.broadcasted_iota(jnp.int32, (amount, places), 0).astype(F32)
    index_v[...] = jnp.sum(jnp.where(hit, order, 0.0), axis=0, keepdims=True).astype(jnp.int32)
    target = column(slot_ref[...].astype(F32) - SLOTS, places)
    named = jnp.sum(jnp.where(hit, target, 0.0), axis=0, keepdims=True) + SLOTS
    info = jnp.concatenate(
        [named[:, k * count : (k + 1) * count] for k in range(CAP)] + [jnp.zeros((8 - CAP, count), F32)],
        axis=0,
    )
    info_ref[:, 0, :] = jnp.concatenate([info.T, jnp.zeros((count, LANES - 8), F32)], axis=1)
    near = nbr_ref[...] - (me - 1) * BLK
    near = jnp.where(near < 0, near + BLK * count, near)
    near = jnp.where(near >= BLK * count, near - BLK * count, near)
    lidx_v[0:K, 0:BLK] = jnp.minimum(near, 3 * BLK - 1)
    tables = [
        pltpu.make_async_copy(index_v, index_ref, table_sem.at[0]),
        pltpu.make_async_copy(lidx_v, lidx_ref, table_sem.at[1]),
    ]
    for c in tables:
        c.start()

    subs = [(g, lax.rem(s + i, members)) for i in range(1, members)]
    grps = [(lax.rem(g + i, groups), s) for i in range(1, groups)]

    for h in range(2):
        loads[h].wait()
        for c in range(HALF):
            block = jnp.concatenate(
                [
                    tiles[0, pl.ds(c * TS, TS), pl.ds(h * LANES, LANES)],
                    tiles[1, pl.ds(c * TS, TS), pl.ds(h * LANES, LANES)],
                ],
                axis=0,
            )
            packed[pl.ds(h * LANES, LANES), c, :] = block.T

    def tile(position):
        return packed[jnp.clip(index_ref[0, position], 0, amount - 1)][:HALF]

    for c in tables:
        c.wait()
    pl.semaphore_wait(barrier, count - 1)

    def remote(src, dst, send, recv, peer):
        return pltpu.make_async_remote_copy(
            src_ref=src, dst_ref=dst, send_sem=send, recv_sem=recv,
            device_id=peer, device_id_type=MESH,
        )

    def piece(p):
        return pl.ds(p * (ROWS // PIECES), ROWS // PIECES)

    def send_halo(src, halo, n, p):
        copies = [
            remote(
                src.at[:, piece(p)], halo.at[0, :, piece(p)],
                halo_send.at[n, 0, p], halo_recv.at[n, 0, p], device(after),
            ),
            remote(
                src.at[:, piece(p)], halo.at[1, :, piece(p)],
                halo_send.at[n, 1, p], halo_recv.at[n, 1, p], device(before),
            ),
        ]
        for c in copies:
            c.start()
        return copies

    def send_sub(src, got, sends, recvs, n):
        copies = [
            remote(src, got.at[n, s], sends.at[n, i], recvs.at[n, i], peer)
            for i, peer in enumerate(subs)
        ]
        for c in copies:
            c.start()
        return copies

    def send_grp(src, n):
        copies = [
            remote(src, grp_got.at[n, g], grp_send.at[n, i], grp_recv.at[n, i], peer)
            for i, peer in enumerate(grps)
        ]
        for c in copies:
            c.start()
        return copies

    def take(copies):
        for c in copies:
            c.wait_recv()

    def sum_sub(n):
        acc = sub_got[n, 0]
        for i in range(1, members):
            acc = acc + sub_got[n, i]
        return acc

    def sum_grp(n):
        acc = grp_got[n, 0]
        for i in range(1, groups):
            acc = acc + grp_got[n, i]
        return acc

    def columns(q):
        return pl.ds(pl.multiple_of(q * LANES, LANES), LANES)

    def put_pair(base, q, x):
        even, odd = spread(x)
        stack[base + 2 * q] = split(even)
        stack[base + 2 * q + 1] = split(odd)


    def info_copy(i):
        other, place = peer_of(i)
        return remote(info_ref.at[other], info_got.at[me], info_send, info_recv, place)

    def send_info(i, carry):
        info_copy(i).start()
        return carry

    landing = pl.ds(pl.multiple_of(me * PITCH, 8), HALF)

    def send_tile(k, i):
        other, place = peer_of(i)
        sent[k, other] = tile(k * count + other)
        remote(sent.at[k, other], got.at[k, landing], tile_send.at[k], tile_recv.at[k], place).start()

    def send_tiles(k):
        def send(i, carry):
            send_tile(k, i)
            return carry

        lax.fori_loop(0, count - 1, send, 0)

    def bulk(ref, send, recv):
        part = ref.at[pl.ds(0, count - 1)]
        return remote(part, part, send, recv, device(after))

    def arrived(k):
        part = got.at[k, pl.ds(0, (count - 1) * HALF)]
        remote(part, part, tile_send.at[k], tile_recv.at[k], device(after)).wait_recv()

    for k in range(CAP):
        got[k, landing] = tile(k * count + me)
    info_got[me] = info_ref[me]
    send_tiles(0)
    lax.fori_loop(0, count - 1, send_info, 0)
    send_tiles(1)

    def own0(q, carry):
        put_pair(BLK, q, start_ref[:, columns(q)])
        return carry

    lax.fori_loop(0, PAIRS, own0, 0, unroll=2)

    bulk(info_got, info_send, info_recv).wait_recv()
    slots = info_got[:, 0, :].T
    slot_iota = lax.broadcasted_iota(jnp.int32, (SLOTS, count), 0).astype(F32)

    def hot_of(k):
        hot = (slot_iota == slots[k : k + 1]).astype(F32).astype(BF16)
        return jnp.concatenate([hot, hot], axis=1)

    def add(k, hot, c):
        new = dot(hot, split(got[k, pl.ds(c, count, stride=PITCH), :]), NN)
        at = pl.ds(pl.multiple_of(c * DEPTH, 8), SLOTS)
        total[at] = new if k == 0 else total[at] + new

    for k in range(2, CAP):
        arrived(k - 2)
        hot = hot_of(k - 2)

        def both(c, carry, k=k, hot=hot):
            for j in range(count // HALF):
                i = c * (count // HALF) + j
                if j < count // HALF - 1:
                    send_tile(k, i)
                else:
                    @pl.when(i < count - 1)
                    def _():
                        send_tile(k, i)
            add(k - 2, hot, c)
            return carry

        lax.fori_loop(0, HALF, both, 0)

    halo = [send_halo(start_ref, halo0, 0, p) for p in range(PIECES)]
    started = sum(halo, [])
    for k in range(CAP - 2, CAP):
        arrived(k)
        hot = hot_of(k)

        def one(c, carry, k=k, hot=hot):
            add(k, hot, c)
            return carry

        lax.fori_loop(0, HALF, one, 0, unroll=8)

    low = low_lanes((HALF, LANES))
    row = lax.broadcasted_iota(jnp.int32, (HALF, LANES), 0)
    lane = lax.broadcasted_iota(jnp.int32, (HALF, LANES), 1)
    on_diagonal = (lane % TS) == row + HALF * (lane // TS)

    def form(q, carry):
        both = shift_ref[pl.ds(q, 1)]
        shift_of = [jnp.where(low[:1], both, roll(both)), jnp.where(low[:1], roll(both), both)]
        for b in range(2):
            r = 2 * q + b
            t = [total[pl.ds(r * K + k, HALF, stride=DEPTH), :] for k in range(K)]
            t[0] = t[0] + jnp.where(on_diagonal, shift_of[b], 0.0)
            for j in range(3):
                x = t[2 * j]
                y = t[2 * j + 1] if 2 * j + 1 < K else jnp.zeros_like(x)
                pair = jnp.concatenate([jnp.where(low, x, roll(y)), jnp.where(low, roll(x), y)], axis=0)
                op[r, :, pl.ds(j * LANES, LANES)] = split(pair)
        return carry

    lax.fori_loop(0, PAIRS, form, 0, unroll=2)

    def spread_halo(ref, side, q, carry):
        put_pair(side * 2 * BLK, q, ref[side, :, columns(q)])
        return carry

    def spread_halos(ref, halo):
        for p in range(PIECES):
            take(halo[p])
            for side in range(2):
                lax.fori_loop(
                    p * (PAIRS // PIECES), (p + 1) * (PAIRS // PIECES),
                    functools.partial(spread_halo, ref, side), 0, unroll=4,
                )

    spread_halos(halo0, halo)

    masks = half_masks()

    def product(out, q, carry):
        even = apply_row(stack, lidx_ref, op, 2 * q, masks)
        odd = apply_row(stack, lidx_ref, op, 2 * q + 1, masks)
        out[:, columns(q)] = jnp.where(low_lanes(even.shape), even, odd)
        return carry

    def products(out, halo, n):
        copies, gram = [], None
        for p in range(PIECES):
            lax.fori_loop(
                p * (PAIRS // PIECES), (p + 1) * (PAIRS // PIECES),
                functools.partial(product, out), 0, unroll=4,
            )
            copies.append(send_halo(out, halo, n, p))
            parts = gram_parts(out[:, piece(p)])
            part = dot(parts, parts, NT)
            gram = part if gram is None else gram + part
        return copies, pack(fold_gram(gram))

    halo, partial[0] = products(x1, halo1, 1)
    started += sum(halo, [])

    first = send_grp(partial.at[0], 0)
    grp_got[0, g] = partial[0]

    def own1(q, carry):
        put_pair(BLK, q, x1[:, columns(q)])
        return carry

    lax.fori_loop(0, PAIRS, own1, 0, unroll=4)
    spread_halos(halo1, halo)
    take(first)
    partial[1] = sum_grp(0)
    second = send_sub(partial.at[1], sub_got, sub_send, sub_recv, 0)
    sub_got[0, s] = partial[1]
    started += first + second

    halo, partial[2] = products(z, halo2, 2)
    started += sum(halo, [])
    third = send_grp(partial.at[2], 1)
    grp_got[1, g] = partial[2]

    take(second)
    inverse1 = inverse_factor(sum_sub(0) / total_rows)
    wide1 = wide(inverse1)

    take(third)
    partial[3] = sum_grp(1)
    fourth = send_sub(partial.at[3], sub_got, sub_send, sub_recv, 1)
    sub_got[1, s] = partial[3]
    started += third + fourth

    def own2(q, carry):
        x = times(wide1, split(z[:, columns(q)]))
        halves[:, columns(q)] = split(x)
        put_pair(BLK, q, x)
        return carry

    lax.fori_loop(0, PAIRS, own2, 0, unroll=4)

    def ext2(side, q, carry):
        put_pair(side * 2 * BLK, q, times(wide1, split(halo2[side, :, columns(q)])))
        return carry

    for p in range(PIECES):
        take(halo[p])
        for side in range(2):
            lax.fori_loop(
                p * (PAIRS // PIECES), (p + 1) * (PAIRS // PIECES),
                functools.partial(ext2, side), 0, unroll=4,
            )

    low, high = masks

    def project(q, carry):
        rows = []
        for r in (2 * q, 2 * q + 1):
            b = blocks_of(stack, lidx_ref, r)
            at = [lidx_ref[k, r] // BLK for k in range(K)]
            lefts = []
            for o in range(3):
                c = [(at[k] == o).astype(F32) for k in range(K)]
                m = [(low.astype(F32) * c[k] if k % 2 == 0 else high.astype(F32) * c[k]).astype(BF16) for k in range(K)]
                lefts.append(
                    jnp.concatenate([b[0] * m[0] + b[1] * m[1], b[2] * m[2] + b[3] * m[3], b[4] * m[4]], axis=1)
                )
            out = dot(jnp.concatenate(lefts, axis=0), op[r], NT)
            rows.append([fold(out[o * 2 * TS : (o + 1) * 2 * TS]) for o in range(3)])
        for o in range(3):
            x = jnp.where(low_lanes((TS, LANES)), rows[0][o], rows[1][o])
            mapped[o, :, columns(q)] = split(x)
        return carry

    lax.fori_loop(0, PAIRS, project, 0, unroll=4)
    h = [fold(dot(halves[...], mapped[o], NT)) for o in range(3)]
    is_first = (s == 0).astype(F32)
    is_last = (s == members - 1).astype(F32)
    term[0:HALF] = pack(is_first * h[0])
    term[HALF : 2 * HALF] = pack(h[1] + (1.0 - is_first) * h[0] + (1.0 - is_last) * h[2])
    term[2 * HALF : 3 * HALF] = pack(is_last * h[2])
    terms = [
        remote(term, final.at[s], term_send.at[i], term_recv.at[i], peer)
        for i, peer in enumerate(subs)
    ]
    for c in terms:
        c.start()
    final[s] = term[...]
    started += terms

    take(fourth)
    packed_gram = sum_sub(1) / total_rows
    square = inverse1[:, :TS]
    gram = jnp.concatenate([packed_gram[:, :TS], roll(packed_gram)[:, :TS]], axis=0)
    gram = exact(exact(square, gram, NN), square, NT)
    inverse_ref[...] = inverse_factor(jnp.concatenate([gram[:HALF], gram[HALF:]], axis=1))
    take(terms)
    acc = final[0]
    for i in range(1, members):
        acc = acc + final[i]
    acc_ref[...] = acc
    for c in started:
        c.wait_send()
    for c in [bulk(info_got, info_send, info_recv)] + [
        bulk(sent.at[k], tile_send.at[k], tile_recv.at[k]) for k in range(CAP)
    ]:
        c.wait_send()


def whole(owner, slot, nbr, shift, start, x, groups, members, total_rows):
    vmem = pl.BlockSpec(memory_space=pltpu.VMEM)
    dma = pltpu.SemaphoreType.DMA
    count = groups * members
    tiles = x.shape[2]
    return pl.pallas_call(
        functools.partial(whole_kernel, groups, members, total_rows),
        out_shape=(
            jax.ShapeDtypeStruct((2 * TS, ROWS), BF16),
            jax.ShapeDtypeStruct((TS, LANES), F32),
            jax.ShapeDtypeStruct((3 * HALF, LANES), F32),
        ),
        in_specs=[vmem, vmem, vmem, vmem, vmem, pl.BlockSpec(memory_space=pl.ANY)],
        out_specs=(vmem, vmem, vmem),
        scratch_shapes=[
            pltpu.VMEM((1, CAP * count), jnp.int32),
            pltpu.SMEM((1, CAP * count), jnp.int32),
            pltpu.VMEM((8, LANES), jnp.int32),
            pltpu.SMEM((8, LANES), jnp.int32),
            pltpu.VMEM((count, 1, LANES), F32),
            pltpu.VMEM((2, HALF * TS, tiles), F32),
            pltpu.VMEM((tiles, PITCH, LANES), F32),
            pltpu.VMEM((CAP, count, HALF, LANES), F32),
            pltpu.VMEM((CAP, count * PITCH, LANES), F32),
            pltpu.VMEM((count, 1, LANES), F32),
            pltpu.VMEM((HALF * DEPTH, LANES), F32),
            pltpu.VMEM((BLK, 2 * TS, 3 * LANES), BF16),
            pltpu.VMEM((TS, ROWS), F32),
            pltpu.VMEM((3 * BLK, 2 * TS, LANES), BF16),
            pltpu.VMEM((2, TS, ROWS), F32),
            pltpu.VMEM((2, TS, ROWS), F32),
            pltpu.VMEM((2, TS, ROWS), F32),
            pltpu.VMEM((TS, ROWS), F32),
            pltpu.VMEM((3, 2 * TS, ROWS), BF16),
            pltpu.VMEM((2, members, HALF, LANES), F32),
            pltpu.VMEM((2, groups, HALF, LANES), F32),
            pltpu.VMEM((4, HALF, LANES), F32),
            pltpu.VMEM((members, 3 * HALF, LANES), F32),
            pltpu.VMEM((3 * HALF, LANES), F32),
            dma((2,)),
            dma((2,)),
            dma((CAP,)),
            dma((CAP,)),
            dma,
            dma,
            dma((3, 2, PIECES)),
            dma((3, 2, PIECES)),
            dma((2, members - 1)),
            dma((2, members - 1)),
            dma((2, groups - 1)),
            dma((2, groups - 1)),
            dma((members - 1,)),
            dma((members - 1,)),
        ],
        compiler_params=pltpu.CompilerParams(
            collective_id=1, has_side_effects=True, vmem_limit_bytes=60 << 20
        ),
    )(owner, slot, nbr, shift, start, x)


def finish_kernel(groups, members, total_rows, halves_ref, inverse_ref, acc_ref, basis_ref, coarse_ref, tail):
    inverse = inverse_ref[...]
    step = pl.program_id(0)
    basis_ref[...] = times(wide(inverse), halves_ref[...])

    @pl.when(step == 0)
    def _():
        square = inverse[:, :TS]
        sides = []
        for o in range(3):
            packed = acc_ref[o * HALF : (o + 1) * HALF]
            sides.append(jnp.concatenate([packed, roll(packed)], axis=0))
        left = exact(square, jnp.concatenate(sides, axis=1), NN)
        left = jnp.concatenate([left[:, o * LANES : o * LANES + TS] for o in range(3)], axis=0)
        full = exact(left, square, NT) * (groups / total_rows)
        for o in range(3):
            tail[:, o * LANES : o * LANES + TS] = full[o * TS : (o + 1) * TS]
        each = TS // members
        mine = pl.ds(pl.multiple_of(lax.axis_index("sub") * each, each), each)
        for o in range(3):
            coarse_ref[:, o * TS : (o + 1) * TS] = tail[mine, o * LANES : o * LANES + TS]


def finish(halves, inverse, acc, groups, members, total_rows):
    steps = 2
    return pl.pallas_call(
        functools.partial(finish_kernel, groups, members, total_rows),
        out_shape=(
            jax.ShapeDtypeStruct((TS, ROWS), F32),
            jax.ShapeDtypeStruct((TS // members, 3 * TS), F32),
        ),
        grid=(steps,),
        in_specs=[
            pl.BlockSpec((2 * TS, ROWS // steps), lambda i: (0, i)),
            pl.BlockSpec((TS, LANES), lambda i: (0, 0)),
            pl.BlockSpec((3 * HALF, LANES), lambda i: (0, 0)),
        ],
        out_specs=(
            pl.BlockSpec((TS, ROWS // steps), lambda i: (0, i)),
            pl.BlockSpec((TS // members, 3 * TS), lambda i: (0, 0)),
        ),
        scratch_shapes=[pltpu.VMEM((TS, 3 * LANES), F32)],
    )(halves, inverse, acc)


def shards(tiles, owner, slot, nbr, shift, start):
    groups, members = lax.axis_size("grp"), lax.axis_size("sub")
    total_rows = float(ROWS * groups * members)
    count = tiles.shape[0]
    x = tiles.transpose(1, 2, 0).reshape(2, HALF * TS, count)
    halves, inverse, acc = whole(
        owner.T, slot.reshape(1, count), nbr.T, shift.reshape(PAIRS, LANES), start.T, x,
        groups, members, total_rows,
    )
    basis, coarse = finish(halves, inverse, acc, groups, members, total_rows)
    return basis.T, coarse[None]


def solution(mesh):
    placed = (
        P(("grp", "sub"), None, None),
        P(("grp", "sub"), None),
        P(("grp", "sub")),
        P(("grp", "sub"), None),
        P(("grp", "sub")),
        P(("grp", "sub"), None),
    )
    return jax.shard_map(
        shards,
        mesh=mesh,
        in_specs=placed,
        out_specs=(P(("grp", "sub"), None), P("grp", "sub", None)),
        check_vma=False,
    )
```

```python
import functools

import jax
import jax.numpy as jnp
from jax import lax
from jax.experimental import pallas as pl
from jax.experimental.pallas import tpu as pltpu
from jax.sharding import PartitionSpec as P

K = 5
CAP = 4
TS = 64
HALF = 32
PITCH = 40
LANES = 128
BLK = 32
ROWS = BLK * TS
PAIRS = ROWS // LANES
SLOTS = BLK * K
DEPTH = SLOTS + 8
NT = (((1,), (1,)), ((), ()))
NN = (((1,), (0,)), ((), ()))
PIECES = 4
STRIDE = 53
SHIFT = 76
MESH = pl.DeviceIdType.MESH
F32 = jnp.float32
BF16 = jnp.bfloat16


def dot(a, b, dims):
    return lax.dot_general(a, b, dims, preferred_element_type=F32)


def exact(a, b, dims):
    return lax.dot_general(a, b, dims, precision=lax.Precision.HIGHEST, preferred_element_type=F32)


def roll(x):
    return pltpu.roll(x, TS, axis=1)


def low_lanes(shape):
    return lax.broadcasted_iota(jnp.int32, shape, 1) < TS


def split(x):
    hi = x.astype(BF16)
    lo = (x - hi.astype(F32)).astype(BF16)
    return jnp.concatenate([hi, lo], axis=0)


def fold(out):
    t = out[:TS] + out[TS:]
    return t + roll(t)


def gram_parts(x):
    hi = x.astype(BF16)
    rest = x - hi.astype(F32)
    mid = rest.astype(BF16)
    lo = (rest - mid.astype(F32)).astype(BF16)
    return jnp.concatenate([hi, mid, lo, jnp.zeros_like(lo)], axis=0)


def fold_gram(out):
    t = out[:TS] + out[TS : 2 * TS] + out[2 * TS : 3 * TS]
    t = t[:, :LANES] + t[:, LANES:]
    return t + roll(t)


def spread(x):
    low = low_lanes(x.shape)
    r = roll(x)
    return jnp.where(low, x, r), jnp.where(low, r, x)


def pack(x):
    return jnp.where(low_lanes((HALF, LANES)), x[:HALF], x[HALF:])


def half_masks():
    low = low_lanes((1, LANES)).astype(F32)
    return low.astype(BF16), (1.0 - low).astype(BF16)


def blocks_of(stack_ref, lidx_ref, r):
    return [stack_ref[jnp.clip(lidx_ref[k, r], 0, 3 * BLK - 1)] for k in range(K)]


def apply_row(stack_ref, lidx_ref, op_ref, r, masks):
    low, high = masks
    b = blocks_of(stack_ref, lidx_ref, r)
    left = jnp.concatenate([b[0] * low + b[1] * high, b[2] * low + b[3] * high, b[4]], axis=1)
    return fold(dot(left, op_ref[r], NT))


def inverse_factor(gram):
    lane = lax.broadcasted_iota(jnp.int32, (8, LANES), 1)
    row = lax.broadcasted_iota(jnp.int32, (8, LANES), 0)
    rolled = roll(gram)
    blocks = []
    for b in range(TS // 8):
        source = gram if b < 4 else rolled
        part = source[8 * (b % 4) : 8 * (b % 4) + 8]
        unit = (lane == row + (TS + 8 * b)).astype(F32)
        blocks.append(jnp.where(lane < TS, part, unit))
    for jb in range(TS // 8):
        cols = {
            b: [
                jnp.broadcast_to(blocks[b][:, 8 * jb + m : 8 * jb + m + 1], (8, LANES))
                for m in range(8)
            ]
            for b in range(jb, TS // 8)
        }
        e = [[jnp.broadcast_to(cols[jb][m][i : i + 1], (8, LANES)) for m in range(i + 1)] for i in range(8)]
        rows = [jnp.broadcast_to(blocks[jb][i : i + 1], (8, LANES)) for i in range(8)]
        l = [[None] * 8 for _ in range(8)]
        inv = []
        for m in range(8):
            inv.append(1.0 / e[m][m])
            for i in range(m + 1, 8):
                l[i][m] = e[i][m] * inv[m]
            for i in range(m + 1, 8):
                for k in range(m + 1, i + 1):
                    e[i][k] = e[i][k] - l[i][m] * e[k][m]
                rows[i] = rows[i] - l[i][m] * rows[m]
        solved = [None] * 8
        for m in reversed(range(8)):
            acc = rows[m] * inv[m]
            for i in reversed(range(m + 1, 8)):
                acc = acc - l[i][m] * solved[i]
            solved[m] = acc
        for b in range(jb + 1, TS // 8):
            acc = [cols[b][m] * solved[m] for m in range(8)]
            while len(acc) > 1:
                acc = [acc[i] + acc[i + 1] for i in range(0, len(acc), 2)]
            blocks[b] = blocks[b] - acc[0]
        done = rows[0] * lax.rsqrt(e[0][0])
        for m in range(1, 8):
            done = jnp.where(row == m, rows[m] * lax.rsqrt(e[m][m]), done)
        blocks[jb] = done
    a = jnp.concatenate(blocks, axis=0)
    return jnp.where(low_lanes(a.shape), roll(a), a)


def wide(inverse):
    hi = inverse.astype(BF16)
    lo = (inverse - hi.astype(F32)).astype(BF16)
    return jnp.concatenate([hi, lo], axis=1)


def times(inverse, x):
    return dot(inverse, jnp.concatenate([x, x], axis=0), NN)


def whole_kernel(
    groups, members, total_rows,
    owner_ref, slot_ref, nbr_ref, shift_ref, start_ref, x_ref,
    halves, inverse_ref, acc_ref,
    index_v, index_ref, lidx_v, lidx_ref, info_ref, tiles, packed, sent, got, info_got, total, op, x1,
    stack, halo0, halo1, halo2, z, mapped, sub_got, grp_got, partial, final, term,
    load_sem, table_sem, tile_send, tile_recv, info_send, info_recv,
    halo_send, halo_recv, sub_send, sub_recv, grp_send, grp_recv, term_send, term_recv,
):
    g, s = lax.axis_index("grp"), lax.axis_index("sub")
    me = g * members + s
    count = groups * members
    after, before = lax.rem(me + 1, count), lax.rem(me + count - 1, count)

    def device(index):
        return (index // members, lax.rem(index, members))

    def peer_of(i):
        other = jnp.bitwise_xor(me, lax.rem(i * STRIDE + me * SHIFT, count - 1) + 1)
        return other, device(other)

    loads = [
        pltpu.make_async_copy(
            x_ref.at[:, :, pl.ds(h * LANES, LANES)], tiles.at[:, :, pl.ds(h * LANES, LANES)], load_sem.at[h]
        )
        for h in range(2)
    ]
    for c in loads:
        c.start()

    barrier = pltpu.get_barrier_semaphore()

    def greet(i, carry):
        pl.semaphore_signal(barrier, inc=1, device_id=peer_of(i)[1], device_id_type=MESH)
        return carry

    lax.fori_loop(0, count - 1, greet, 0)

    amount = owner_ref.shape[1]
    places = CAP * count

    def column(x, width):
        tall = jnp.broadcast_to(x, (8, x.shape[1])).T
        return jnp.broadcast_to(tall[:, :1], (x.shape[1], width))

    dest = owner_ref[...].astype(F32)
    down = lax.broadcasted_iota(jnp.int32, (amount, amount), 0)
    across = lax.broadcasted_iota(jnp.int32, (amount, amount), 1)
    earlier = (column(dest, amount) == dest) & (down < across)
    rank = jnp.sum(jnp.where(earlier, 1.0, 0.0), axis=0, keepdims=True)
    place = column(rank * count + dest, places)
    hit = place == lax.broadcasted_iota(jnp.int32, (amount, places), 1).astype(F32)
    order = lax.broadcasted_iota(jnp.int32, (amount, places), 0).astype(F32)
    index_v[...] = jnp.sum(jnp.where(hit, order, 0.0), axis=0, keepdims=True).astype(jnp.int32)
    target = column(slot_ref[...].astype(F32) - SLOTS, places)
    named = jnp.sum(jnp.where(hit, target, 0.0), axis=0, keepdims=True) + SLOTS
    info = jnp.concatenate(
        [named[:, k * count : (k + 1) * count] for k in range(CAP)] + [jnp.zeros((8 - CAP, count), F32)],
        axis=0,
    )
    info_ref[:, 0, :] = jnp.concatenate([info.T, jnp.zeros((count, LANES - 8), F32)], axis=1)
    near = nbr_ref[...] - (me - 1) * BLK
    near = jnp.where(near < 0, near + BLK * count, near)
    near = jnp.where(near >= BLK * count, near - BLK * count, near)
    lidx_v[0:K, 0:BLK] = jnp.minimum(near, 3 * BLK - 1)
    tables = [
        pltpu.make_async_copy(index_v, index_ref, table_sem.at[0]),
        pltpu.make_async_copy(lidx_v, lidx_ref, table_sem.at[1]),
    ]
    for c in tables:
        c.start()

    subs = [(g, lax.rem(s + i, members)) for i in range(1, members)]
    grps = [(lax.rem(g + i, groups), s) for i in range(1, groups)]

    for h in range(2):
        loads[h].wait()
        for c in range(HALF):
            block = jnp.concatenate(
                [
                    tiles[0, pl.ds(c * TS, TS), pl.ds(h * LANES, LANES)],
                    tiles[1, pl.ds(c * TS, TS), pl.ds(h * LANES, LANES)],
                ],
                axis=0,
            )
            packed[pl.ds(h * LANES, LANES), c, :] = block.T

    def tile(position):
        return packed[jnp.clip(index_ref[0, position], 0, amount - 1)][:HALF]

    for c in tables:
        c.wait()
    pl.semaphore_wait(barrier, count - 1)

    def remote(src, dst, send, recv, peer):
        return pltpu.make_async_remote_copy(
            src_ref=src, dst_ref=dst, send_sem=send, recv_sem=recv,
            device_id=peer, device_id_type=MESH,
        )

    def piece(p):
        return pl.ds(p * (ROWS // PIECES), ROWS // PIECES)

    def send_halo(src, halo, n, p):
        copies = [
            remote(
                src.at[:, piece(p)], halo.at[0, :, piece(p)],
                halo_send.at[n, 0, p], halo_recv.at[n, 0, p], device(after),
            ),
            remote(
                src.at[:, piece(p)], halo.at[1, :, piece(p)],
                halo_send.at[n, 1, p], halo_recv.at[n, 1, p], device(before),
            ),
        ]
        for c in copies:
            c.start()
        return copies

    def send_sub(src, got, sends, recvs, n):
        copies = [
            remote(src, got.at[n, s], sends.at[n, i], recvs.at[n, i], peer)
            for i, peer in enumerate(subs)
        ]
        for c in copies:
            c.start()
        return copies

    def send_grp(src, n):
        copies = [
            remote(src, grp_got.at[n, g], grp_send.at[n, i], grp_recv.at[n, i], peer)
            for i, peer in enumerate(grps)
        ]
        for c in copies:
            c.start()
        return copies

    def take(copies):
        for c in copies:
            c.wait_recv()

    def sum_sub(n):
        acc = sub_got[n, 0]
        for i in range(1, members):
            acc = acc + sub_got[n, i]
        return acc

    def sum_grp(n):
        acc = grp_got[n, 0]
        for i in range(1, groups):
            acc = acc + grp_got[n, i]
        return acc

    def columns(q):
        return pl.ds(pl.multiple_of(q * LANES, LANES), LANES)

    def put_pair(base, q, x):
        even, odd = spread(x)
        stack[base + 2 * q] = split(even)
        stack[base + 2 * q + 1] = split(odd)


    def info_copy(i):
        other, place = peer_of(i)
        return remote(info_ref.at[other], info_got.at[me], info_send, info_recv, place)

    def send_info(i, carry):
        info_copy(i).start()
        return carry

    landing = pl.ds(pl.multiple_of(me * PITCH, 8), HALF)

    def send_tile(k, i):
        other, place = peer_of(i)
        sent[k, other] = tile(k * count + other)
        remote(sent.at[k, other], got.at[k, landing], tile_send.at[k], tile_recv.at[k], place).start()

    def send_tiles(k):
        def send(i, carry):
            send_tile(k, i)
            return carry

        lax.fori_loop(0, count - 1, send, 0)

    def bulk(ref, send, recv):
        part = ref.at[pl.ds(0, count - 1)]
        return remote(part, part, send, recv, device(after))

    def arrived(k):
        part = got.at[k, pl.ds(0, (count - 1) * HALF)]
        remote(part, part, tile_send.at[k], tile_recv.at[k], device(after)).wait_recv()

    for k in range(CAP):
        got[k, landing] = tile(k * count + me)
    info_got[me] = info_ref[me]
    send_tiles(0)
    lax.fori_loop(0, count - 1, send_info, 0)
    send_tiles(1)

    def own0(q, carry):
        put_pair(BLK, q, start_ref[:, columns(q)])
        return carry

    lax.fori_loop(0, PAIRS, own0, 0, unroll=2)

    bulk(info_got, info_send, info_recv).wait_recv()
    slots = info_got[:, 0, :].T
    slot_iota = lax.broadcasted_iota(jnp.int32, (SLOTS, count), 0).astype(F32)

    def hot_of(k):
        hot = (slot_iota == slots[k : k + 1]).astype(F32).astype(BF16)
        return jnp.concatenate([hot, hot], axis=1)

    def add(k, hot, c):
        new = dot(hot, split(got[k, pl.ds(c, count, stride=PITCH), :]), NN)
        at = pl.ds(pl.multiple_of(c * DEPTH, 8), SLOTS)
        total[at] = new if k == 0 else total[at] + new

    for k in range(2, CAP):
        arrived(k - 2)
        hot = hot_of(k - 2)

        def both(c, carry, k=k, hot=hot):
            for j in range(count // HALF):
                i = c * (count // HALF) + j
                if j < count // HALF - 1:
                    send_tile(k, i)
                else:
                    @pl.when(i < count - 1)
                    def _():
                        send_tile(k, i)
            add(k - 2, hot, c)
            return carry

        lax.fori_loop(0, HALF, both, 0)

    halo = [send_halo(start_ref, halo0, 0, p) for p in range(PIECES)]
    started = sum(halo, [])
    for k in range(CAP - 2, CAP):
        arrived(k)
        hot = hot_of(k)

        def one(c, carry, k=k, hot=hot):
            add(k, hot, c)
            return carry

        lax.fori_loop(0, HALF, one, 0, unroll=8)

    low = low_lanes((HALF, LANES))
    row = lax.broadcasted_iota(jnp.int32, (HALF, LANES), 0)
    lane = lax.broadcasted_iota(jnp.int32, (HALF, LANES), 1)
    on_diagonal = (lane % TS) == row + HALF * (lane // TS)

    def form(q, carry):
        both = shift_ref[pl.ds(q, 1)]
        shift_of = [jnp.where(low[:1], both, roll(both)), jnp.where(low[:1], roll(both), both)]
        for b in range(2):
            r = 2 * q + b
            t = [total[pl.ds(r * K + k, HALF, stride=DEPTH), :] for k in range(K)]
            t[0] = t[0] + jnp.where(on_diagonal, shift_of[b], 0.0)
            for j in range(3):
                x = t[2 * j]
                y = t[2 * j + 1] if 2 * j + 1 < K else jnp.zeros_like(x)
                pair = jnp.concatenate([jnp.where(low, x, roll(y)), jnp.where(low, roll(x), y)], axis=0)
                op[r, :, pl.ds(j * LANES, LANES)] = split(pair)
        return carry

    lax.fori_loop(0, PAIRS, form, 0, unroll=2)

    def spread_halo(ref, side, q, carry):
        put_pair(side * 2 * BLK, q, ref[side, :, columns(q)])
        return carry

    def spread_halos(ref, halo):
        for p in range(PIECES):
            take(halo[p])
            for side in range(2):
                lax.fori_loop(
                    p * (PAIRS // PIECES), (p + 1) * (PAIRS // PIECES),
                    functools.partial(spread_halo, ref, side), 0, unroll=4,
                )

    spread_halos(halo0, halo)

    masks = half_masks()

    def product(out, q, carry):
        even = apply_row(stack, lidx_ref, op, 2 * q, masks)
        odd = apply_row(stack, lidx_ref, op, 2 * q + 1, masks)
        out[:, columns(q)] = jnp.where(low_lanes(even.shape), even, odd)
        return carry

    def products(out, halo, n):
        copies, gram = [], None
        for p in range(PIECES):
            lax.fori_loop(
                p * (PAIRS // PIECES), (p + 1) * (PAIRS // PIECES),
                functools.partial(product, out), 0, unroll=4,
            )
            copies.append(send_halo(out, halo, n, p))
            parts = gram_parts(out[:, piece(p)])
            part = dot(parts, parts, NT)
            gram = part if gram is None else gram + part
        return copies, pack(fold_gram(gram))

    halo, partial[0] = products(x1, halo1, 1)
    started += sum(halo, [])

    first = send_grp(partial.at[0], 0)
    grp_got[0, g] = partial[0]

    def own1(q, carry):
        put_pair(BLK, q, x1[:, columns(q)])
        return carry

    lax.fori_loop(0, PAIRS, own1, 0, unroll=4)
    spread_halos(halo1, halo)
    take(first)
    partial[1] = sum_grp(0)
    second = send_sub(partial.at[1], sub_got, sub_send, sub_recv, 0)
    sub_got[0, s] = partial[1]
    started += first + second

    halo, partial[2] = products(z, halo2, 2)
    started += sum(halo, [])
    third = send_grp(partial.at[2], 1)
    grp_got[1, g] = partial[2]

    take(second)
    inverse1 = inverse_factor(sum_sub(0) / total_rows)
    wide1 = wide(inverse1)

    take(third)
    partial[3] = sum_grp(1)
    fourth = send_sub(partial.at[3], sub_got, sub_send, sub_recv, 1)
    sub_got[1, s] = partial[3]
    started += third + fourth

    def own2(q, carry):
        x = times(wide1, split(z[:, columns(q)]))
        halves[:, columns(q)] = split(x)
        put_pair(BLK, q, x)
        return carry

    lax.fori_loop(0, PAIRS, own2, 0, unroll=4)

    def ext2(side, q, carry):
        put_pair(side * 2 * BLK, q, times(wide1, split(halo2[side, :, columns(q)])))
        return carry

    for p in range(PIECES):
        take(halo[p])
        for side in range(2):
            lax.fori_loop(
                p * (PAIRS // PIECES), (p + 1) * (PAIRS // PIECES),
                functools.partial(ext2, side), 0, unroll=4,
            )

    low, high = masks

    def project(q, carry):
        rows = []
        for r in (2 * q, 2 * q + 1):
            b = blocks_of(stack, lidx_ref, r)
            at = [lidx_ref[k, r] // BLK for k in range(K)]
            lefts = []
            for o in range(3):
                c = [(at[k] == o).astype(F32) for k in range(K)]
                m = [(low.astype(F32) * c[k] if k % 2 == 0 else high.astype(F32) * c[k]).astype(BF16) for k in range(K)]
                lefts.append(
                    jnp.concatenate([b[0] * m[0] + b[1] * m[1], b[2] * m[2] + b[3] * m[3], b[4] * m[4]], axis=1)
                )
            out = dot(jnp.concatenate(lefts, axis=0), op[r], NT)
            rows.append([fold(out[o * 2 * TS : (o + 1) * 2 * TS]) for o in range(3)])
        for o in range(3):
            x = jnp.where(low_lanes((TS, LANES)), rows[0][o], rows[1][o])
            mapped[o, :, columns(q)] = split(x)
        return carry

    lax.fori_loop(0, PAIRS, project, 0, unroll=4)
    h = [fold(dot(halves[...], mapped[o], NT)) for o in range(3)]
    is_first = (s == 0).astype(F32)
    is_last = (s == members - 1).astype(F32)
    term[0:HALF] = pack(is_first * h[0])
    term[HALF : 2 * HALF] = pack(h[1] + (1.0 - is_first) * h[0] + (1.0 - is_last) * h[2])
    term[2 * HALF : 3 * HALF] = pack(is_last * h[2])
    terms = [
        remote(term, final.at[s], term_send.at[i], term_recv.at[i], peer)
        for i, peer in enumerate(subs)
    ]
    for c in terms:
        c.start()
    final[s] = term[...]
    started += terms

    take(fourth)
    packed_gram = sum_sub(1) / total_rows
    square = inverse1[:, :TS]
    gram = jnp.concatenate([packed_gram[:, :TS], roll(packed_gram)[:, :TS]], axis=0)
    gram = exact(exact(square, gram, NN), square, NT)
    inverse_ref[...] = inverse_factor(jnp.concatenate([gram[:HALF], gram[HALF:]], axis=1))
    take(terms)
    acc = final[0]
    for i in range(1, members):
        acc = acc + final[i]
    acc_ref[...] = acc
    for c in started:
        c.wait_send()
    for c in [bulk(info_got, info_send, info_recv)] + [
        bulk(sent.at[k], tile_send.at[k], tile_recv.at[k]) for k in range(CAP)
    ]:
        c.wait_send()


def whole(owner, slot, nbr, shift, start, x, groups, members, total_rows):
    vmem = pl.BlockSpec(memory_space=pltpu.VMEM)
    dma = pltpu.SemaphoreType.DMA
    count = groups * members
    tiles = x.shape[2]
    return pl.pallas_call(
        functools.partial(whole_kernel, groups, members, total_rows),
        out_shape=(
            jax.ShapeDtypeStruct((2 * TS, ROWS), BF16),
            jax.ShapeDtypeStruct((TS, LANES), F32),
            jax.ShapeDtypeStruct((3 * HALF, LANES), F32),
        ),
        in_specs=[vmem, vmem, vmem, vmem, vmem, pl.BlockSpec(memory_space=pl.ANY)],
        out_specs=(vmem, vmem, vmem),
        scratch_shapes=[
            pltpu.VMEM((1, CAP * count), jnp.int32),
            pltpu.SMEM((1, CAP * count), jnp.int32),
            pltpu.VMEM((8, LANES), jnp.int32),
            pltpu.SMEM((8, LANES), jnp.int32),
            pltpu.VMEM((count, 1, LANES), F32),
            pltpu.VMEM((2, HALF * TS, tiles), F32),
            pltpu.VMEM((tiles, PITCH, LANES), F32),
            pltpu.VMEM((CAP, count, HALF, LANES), F32),
            pltpu.VMEM((CAP, count * PITCH, LANES), F32),
            pltpu.VMEM((count, 1, LANES), F32),
            pltpu.VMEM((HALF * DEPTH, LANES), F32),
            pltpu.VMEM((BLK, 2 * TS, 3 * LANES), BF16),
            pltpu.VMEM((TS, ROWS), F32),
            pltpu.VMEM((3 * BLK, 2 * TS, LANES), BF16),
            pltpu.VMEM((2, TS, ROWS), F32),
            pltpu.VMEM((2, TS, ROWS), F32),
            pltpu.VMEM((2, TS, ROWS), F32),
            pltpu.VMEM((TS, ROWS), F32),
            pltpu.VMEM((3, 2 * TS, ROWS), BF16),
            pltpu.VMEM((2, members, HALF, LANES), F32),
            pltpu.VMEM((2, groups, HALF, LANES), F32),
            pltpu.VMEM((4, HALF, LANES), F32),
            pltpu.VMEM((members, 3 * HALF, LANES), F32),
            pltpu.VMEM((3 * HALF, LANES), F32),
            dma((2,)),
            dma((2,)),
            dma((CAP,)),
            dma((CAP,)),
            dma,
            dma,
            dma((3, 2, PIECES)),
            dma((3, 2, PIECES)),
            dma((2, members - 1)),
            dma((2, members - 1)),
            dma((2, groups - 1)),
            dma((2, groups - 1)),
            dma((members - 1,)),
            dma((members - 1,)),
        ],
        compiler_params=pltpu.CompilerParams(
            collective_id=1, has_side_effects=True, vmem_limit_bytes=60 << 20
        ),
    )(owner, slot, nbr, shift, start, x)


def finish_kernel(groups, members, total_rows, halves_ref, inverse_ref, acc_ref, basis_ref, coarse_ref, tail):
    inverse = inverse_ref[...]
    step = pl.program_id(0)
    basis_ref[...] = times(wide(inverse), halves_ref[...])

    @pl.when(step == 0)
    def _():
        square = inverse[:, :TS]
        sides = []
        for o in range(3):
            packed = acc_ref[o * HALF : (o + 1) * HALF]
            sides.append(jnp.concatenate([packed, roll(packed)], axis=0))
        left = exact(square, jnp.concatenate(sides, axis=1), NN)
        left = jnp.concatenate([left[:, o * LANES : o * LANES + TS] for o in range(3)], axis=0)
        full = exact(left, square, NT) * (groups / total_rows)
        for o in range(3):
            tail[:, o * LANES : o * LANES + TS] = full[o * TS : (o + 1) * TS]
        each = TS // members
        mine = pl.ds(pl.multiple_of(lax.axis_index("sub") * each, each), each)
        for o in range(3):
            coarse_ref[:, o * TS : (o + 1) * TS] = tail[mine, o * LANES : o * LANES + TS]


def finish(halves, inverse, acc, groups, members, total_rows):
    steps = 2
    return pl.pallas_call(
        functools.partial(finish_kernel, groups, members, total_rows),
        out_shape=(
            jax.ShapeDtypeStruct((TS, ROWS), F32),
            jax.ShapeDtypeStruct((TS // members, 3 * TS), F32),
        ),
        grid=(steps,),
        in_specs=[
            pl.BlockSpec((2 * TS, ROWS // steps), lambda i: (0, i)),
            pl.BlockSpec((TS, LANES), lambda i: (0, 0)),
            pl.BlockSpec((3 * HALF, LANES), lambda i: (0, 0)),
        ],
        out_specs=(
            pl.BlockSpec((TS, ROWS // steps), lambda i: (0, i)),
            pl.BlockSpec((TS // members, 3 * TS), lambda i: (0, 0)),
        ),
        scratch_shapes=[pltpu.VMEM((TS, 3 * LANES), F32)],
    )(halves, inverse, acc)


def shards(tiles, owner, slot, nbr, shift, start):
    groups, members = lax.axis_size("grp"), lax.axis_size("sub")
    total_rows = float(ROWS * groups * members)
    count = tiles.shape[0]
    x = tiles.transpose(1, 2, 0).reshape(2, HALF * TS, count)
    halves, inverse, acc = whole(
        owner.T, slot.reshape(1, count), nbr.T, shift.reshape(PAIRS, LANES), start.T, x,
        groups, members, total_rows,
    )
    basis, coarse = finish(halves, inverse, acc, groups, members, total_rows)
    return basis.T, coarse[None]


def solution(mesh):
    placed = (
        P(("grp", "sub"), None, None),
        P(("grp", "sub"), None),
        P(("grp", "sub")),
        P(("grp", "sub"), None),
        P(("grp", "sub")),
        P(("grp", "sub"), None),
    )
    return jax.shard_map(
        shards,
        mesh=mesh,
        in_specs=placed,
        out_specs=(P(("grp", "sub"), None), P("grp", "sub", None)),
        check_vma=False,
    )
```

```python
import functools

import jax
import jax.numpy as jnp
from jax import lax
from jax.experimental import pallas as pl
from jax.experimental.pallas import tpu as pltpu
from jax.sharding import PartitionSpec as P

K = 5
CAP = 4
TS = 64
HALF = 32
PITCH = 40
LANES = 128
BLK = 32
ROWS = BLK * TS
PAIRS = ROWS // LANES
SLOTS = BLK * K
DEPTH = SLOTS + 8
NT = (((1,), (1,)), ((), ()))
NN = (((1,), (0,)), ((), ()))
PIECES = 4
STRIDE = 53
SHIFT = 76
MESH = pl.DeviceIdType.MESH
F32 = jnp.float32
BF16 = jnp.bfloat16


def dot(a, b, dims):
    return lax.dot_general(a, b, dims, preferred_element_type=F32)


def exact(a, b, dims):
    return lax.dot_general(a, b, dims, precision=lax.Precision.HIGHEST, preferred_element_type=F32)


def roll(x):
    return pltpu.roll(x, TS, axis=1)


def low_lanes(shape):
    return lax.broadcasted_iota(jnp.int32, shape, 1) < TS


def split(x):
    hi = x.astype(BF16)
    lo = (x - hi.astype(F32)).astype(BF16)
    return jnp.concatenate([hi, lo], axis=0)


def fold(out):
    t = out[:TS] + out[TS:]
    return t + roll(t)


def gram_parts(x):
    hi = x.astype(BF16)
    rest = x - hi.astype(F32)
    mid = rest.astype(BF16)
    lo = (rest - mid.astype(F32)).astype(BF16)
    return jnp.concatenate([hi, mid, lo, jnp.zeros_like(lo)], axis=0)


def fold_gram(out):
    t = out[:TS] + out[TS : 2 * TS] + out[2 * TS : 3 * TS]
    t = t[:, :LANES] + t[:, LANES:]
    return t + roll(t)


def spread(x):
    low = low_lanes(x.shape)
    r = roll(x)
    return jnp.where(low, x, r), jnp.where(low, r, x)


def pack(x):
    return jnp.where(low_lanes((HALF, LANES)), x[:HALF], x[HALF:])


def half_masks():
    low = low_lanes((1, LANES)).astype(F32)
    return low.astype(BF16), (1.0 - low).astype(BF16)


def blocks_of(stack_ref, lidx_ref, r):
    return [stack_ref[jnp.clip(lidx_ref[k, r], 0, 3 * BLK - 1)] for k in range(K)]


def apply_row(stack_ref, lidx_ref, op_ref, r, masks):
    low, high = masks
    b = blocks_of(stack_ref, lidx_ref, r)
    left = jnp.concatenate([b[0] * low + b[1] * high, b[2] * low + b[3] * high, b[4]], axis=1)
    return fold(dot(left, op_ref[r], NT))


def inverse_factor(gram):
    lane = lax.broadcasted_iota(jnp.int32, (8, LANES), 1)
    row = lax.broadcasted_iota(jnp.int32, (8, LANES), 0)
    rolled = roll(gram)
    blocks = []
    for b in range(TS // 8):
        source = gram if b < 4 else rolled
        part = source[8 * (b % 4) : 8 * (b % 4) + 8]
        unit = (lane == row + (TS + 8 * b)).astype(F32)
        blocks.append(jnp.where(lane < TS, part, unit))
    for jb in range(TS // 8):
        cols = {
            b: [
                jnp.broadcast_to(blocks[b][:, 8 * jb + m : 8 * jb + m + 1], (8, LANES))
                for m in range(8)
            ]
            for b in range(jb, TS // 8)
        }
        e = [[jnp.broadcast_to(cols[jb][m][i : i + 1], (8, LANES)) for m in range(i + 1)] for i in range(8)]
        rows = [jnp.broadcast_to(blocks[jb][i : i + 1], (8, LANES)) for i in range(8)]
        l = [[None] * 8 for _ in range(8)]
        inv = []
        for m in range(8):
            inv.append(1.0 / e[m][m])
            for i in range(m + 1, 8):
                l[i][m] = e[i][m] * inv[m]
            for i in range(m + 1, 8):
                for k in range(m + 1, i + 1):
                    e[i][k] = e[i][k] - l[i][m] * e[k][m]
                rows[i] = rows[i] - l[i][m] * rows[m]
        solved = [None] * 8
        for m in reversed(range(8)):
            acc = rows[m] * inv[m]
            for i in reversed(range(m + 1, 8)):
                acc = acc - l[i][m] * solved[i]
            solved[m] = acc
        for b in range(jb + 1, TS // 8):
            acc = [cols[b][m] * solved[m] for m in range(8)]
            while len(acc) > 1:
                acc = [acc[i] + acc[i + 1] for i in range(0, len(acc), 2)]
            blocks[b] = blocks[b] - acc[0]
        done = rows[0] * lax.rsqrt(e[0][0])
        for m in range(1, 8):
            done = jnp.where(row == m, rows[m] * lax.rsqrt(e[m][m]), done)
        blocks[jb] = done
    a = jnp.concatenate(blocks, axis=0)
    return jnp.where(low_lanes(a.shape), roll(a), a)


def wide(inverse):
    hi = inverse.astype(BF16)
    lo = (inverse - hi.astype(F32)).astype(BF16)
    return jnp.concatenate([hi, lo], axis=1)


def times(inverse, x):
    return dot(inverse, jnp.concatenate([x, x], axis=0), NN)


def whole_kernel(
    groups, members, total_rows,
    owner_ref, slot_ref, nbr_ref, shift_ref, start_ref, x_ref,
    halves, inverse_ref, acc_ref,
    index_v, index_ref, lidx_v, lidx_ref, info_ref, tiles, packed, sent, got, info_got, total, op, x1,
    stack, halo0, halo1, halo2, z, mapped, sub_got, grp_got, partial, final, term,
    load_sem, table_sem, tile_send, tile_recv, info_send, info_recv,
    halo_send, halo_recv, sub_send, sub_recv, grp_send, grp_recv, term_send, term_recv,
):
    g, s = lax.axis_index("grp"), lax.axis_index("sub")
    me = g * members + s
    count = groups * members
    after, before = lax.rem(me + 1, count), lax.rem(me + count - 1, count)

    def device(index):
        return (index // members, lax.rem(index, members))

    def peer_of(i):
        other = jnp.bitwise_xor(me, lax.rem(i * STRIDE + me * SHIFT, count - 1) + 1)
        return other, device(other)

    loads = [
        pltpu.make_async_copy(
            x_ref.at[:, :, pl.ds(h * LANES, LANES)], tiles.at[:, :, pl.ds(h * LANES, LANES)], load_sem.at[h]
        )
        for h in range(2)
    ]
    for c in loads:
        c.start()

    barrier = pltpu.get_barrier_semaphore()

    def greet(i, carry):
        pl.semaphore_signal(barrier, inc=1, device_id=peer_of(i)[1], device_id_type=MESH)
        return carry

    lax.fori_loop(0, count - 1, greet, 0)

    amount = owner_ref.shape[1]
    places = CAP * count

    def column(x, width):
        tall = jnp.broadcast_to(x, (8, x.shape[1])).T
        return jnp.broadcast_to(tall[:, :1], (x.shape[1], width))

    dest = owner_ref[...].astype(F32)
    down = lax.broadcasted_iota(jnp.int32, (amount, amount), 0)
    across = lax.broadcasted_iota(jnp.int32, (amount, amount), 1)
    earlier = (column(dest, amount) == dest) & (down < across)
    rank = jnp.sum(jnp.where(earlier, 1.0, 0.0), axis=0, keepdims=True)
    place = column(rank * count + dest, places)
    hit = place == lax.broadcasted_iota(jnp.int32, (amount, places), 1).astype(F32)
    order = lax.broadcasted_iota(jnp.int32, (amount, places), 0).astype(F32)
    index_v[...] = jnp.sum(jnp.where(hit, order, 0.0), axis=0, keepdims=True).astype(jnp.int32)
    target = column(slot_ref[...].astype(F32) - SLOTS, places)
    named = jnp.sum(jnp.where(hit, target, 0.0), axis=0, keepdims=True) + SLOTS
    info = jnp.concatenate(
        [named[:, k * count : (k + 1) * count] for k in range(CAP)] + [jnp.zeros((8 - CAP, count), F32)],
        axis=0,
    )
    info_ref[:, 0, :] = jnp.concatenate([info.T, jnp.zeros((count, LANES - 8), F32)], axis=1)
    near = nbr_ref[...] - (me - 1) * BLK
    near = jnp.where(near < 0, near + BLK * count, near)
    near = jnp.where(near >= BLK * count, near - BLK * count, near)
    lidx_v[0:K, 0:BLK] = jnp.minimum(near, 3 * BLK - 1)
    tables = [
        pltpu.make_async_copy(index_v, index_ref, table_sem.at[0]),
        pltpu.make_async_copy(lidx_v, lidx_ref, table_sem.at[1]),
    ]
    for c in tables:
        c.start()

    subs = [(g, lax.rem(s + i, members)) for i in range(1, members)]
    grps = [(lax.rem(g + i, groups), s) for i in range(1, groups)]

    for h in range(2):
        loads[h].wait()
        for c in range(HALF):
            block = jnp.concatenate(
                [
                    tiles[0, pl.ds(c * TS, TS), pl.ds(h * LANES, LANES)],
                    tiles[1, pl.ds(c * TS, TS), pl.ds(h * LANES, LANES)],
                ],
                axis=0,
            )
            packed[pl.ds(h * LANES, LANES), c, :] = block.T

    def tile(position):
        return packed[jnp.clip(index_ref[0, position], 0, amount - 1)][:HALF]

    for c in tables:
        c.wait()
    pl.semaphore_wait(barrier, count - 1)

    def remote(src, dst, send, recv, peer):
        return pltpu.make_async_remote_copy(
            src_ref=src, dst_ref=dst, send_sem=send, recv_sem=recv,
            device_id=peer, device_id_type=MESH,
        )

    def piece(p):
        return pl.ds(p * (ROWS // PIECES), ROWS // PIECES)

    def send_halo(src, halo, n, p):
        copies = [
            remote(
                src.at[:, piece(p)], halo.at[0, :, piece(p)],
                halo_send.at[n, 0, p], halo_recv.at[n, 0, p], device(after),
            ),
            remote(
                src.at[:, piece(p)], halo.at[1, :, piece(p)],
                halo_send.at[n, 1, p], halo_recv.at[n, 1, p], device(before),
            ),
        ]
        for c in copies:
            c.start()
        return copies

    def send_sub(src, got, sends, recvs, n):
        copies = [
            remote(src, got.at[n, s], sends.at[n, i], recvs.at[n, i], peer)
            for i, peer in enumerate(subs)
        ]
        for c in copies:
            c.start()
        return copies

    def send_grp(src, n):
        copies = [
            remote(src, grp_got.at[n, g], grp_send.at[n, i], grp_recv.at[n, i], peer)
            for i, peer in enumerate(grps)
        ]
        for c in copies:
            c.start()
        return copies

    def take(copies):
        for c in copies:
            c.wait_recv()

    def sum_sub(n):
        acc = sub_got[n, 0]
        for i in range(1, members):
            acc = acc + sub_got[n, i]
        return acc

    def sum_grp(n):
        acc = grp_got[n, 0]
        for i in range(1, groups):
            acc = acc + grp_got[n, i]
        return acc

    def columns(q):
        return pl.ds(pl.multiple_of(q * LANES, LANES), LANES)

    def put_pair(base, q, x):
        even, odd = spread(x)
        stack[base + 2 * q] = split(even)
        stack[base + 2 * q + 1] = split(odd)


    def info_copy(i):
        other, place = peer_of(i)
        return remote(info_ref.at[other], info_got.at[me], info_send, info_recv, place)

    def send_info(i, carry):
        info_copy(i).start()
        return carry

    landing = pl.ds(pl.multiple_of(me * PITCH, 8), HALF)

    def send_tile(k, i):
        other, place = peer_of(i)
        sent[k, other] = tile(k * count + other)
        remote(sent.at[k, other], got.at[k, landing], tile_send.at[k], tile_recv.at[k], place).start()

    def send_tiles(k):
        def send(i, carry):
            send_tile(k, i)
            return carry

        lax.fori_loop(0, count - 1, send, 0)

    def bulk(ref, send, recv):
        part = ref.at[pl.ds(0, count - 1)]
        return remote(part, part, send, recv, device(after))

    def arrived(k):
        part = got.at[k, pl.ds(0, (count - 1) * HALF)]
        remote(part, part, tile_send.at[k], tile_recv.at[k], device(after)).wait_recv()

    for k in range(CAP):
        got[k, landing] = tile(k * count + me)
    info_got[me] = info_ref[me]
    send_tiles(0)
    lax.fori_loop(0, count - 1, send_info, 0)
    send_tiles(1)

    def own0(q, carry):
        put_pair(BLK, q, start_ref[:, columns(q)])
        return carry

    lax.fori_loop(0, PAIRS, own0, 0, unroll=2)

    bulk(info_got, info_send, info_recv).wait_recv()
    slots = info_got[:, 0, :].T
    slot_iota = lax.broadcasted_iota(jnp.int32, (SLOTS, count), 0).astype(F32)

    def hot_of(k):
        hot = (slot_iota == slots[k : k + 1]).astype(F32).astype(BF16)
        return jnp.concatenate([hot, hot], axis=1)

    def add(k, hot, c):
        new = dot(hot, split(got[k, pl.ds(c, count, stride=PITCH), :]), NN)
        at = pl.ds(pl.multiple_of(c * DEPTH, 8), SLOTS)
        total[at] = new if k == 0 else total[at] + new

    for k in range(2, CAP):
        arrived(k - 2)
        hot = hot_of(k - 2)

        def both(c, carry, k=k, hot=hot):
            for j in range(count // HALF):
                i = c * (count // HALF) + j
                if j < count // HALF - 1:
                    send_tile(k, i)
                else:
                    @pl.when(i < count - 1)
                    def _():
                        send_tile(k, i)
            add(k - 2, hot, c)
            return carry

        lax.fori_loop(0, HALF, both, 0)

    halo = [send_halo(start_ref, halo0, 0, p) for p in range(PIECES)]
    started = sum(halo, [])
    for k in range(CAP - 2, CAP):
        arrived(k)
        hot = hot_of(k)

        def one(c, carry, k=k, hot=hot):
            add(k, hot, c)
            return carry

        lax.fori_loop(0, HALF, one, 0, unroll=8)

    low = low_lanes((HALF, LANES))
    row = lax.broadcasted_iota(jnp.int32, (HALF, LANES), 0)
    lane = lax.broadcasted_iota(jnp.int32, (HALF, LANES), 1)
    on_diagonal = (lane % TS) == row + HALF * (lane // TS)

    def form(q, carry):
        both = shift_ref[pl.ds(q, 1)]
        shift_of = [jnp.where(low[:1], both, roll(both)), jnp.where(low[:1], roll(both), both)]
        for b in range(2):
            r = 2 * q + b
            t = [total[pl.ds(r * K + k, HALF, stride=DEPTH), :] for k in range(K)]
            t[0] = t[0] + jnp.where(on_diagonal, shift_of[b], 0.0)
            for j in range(3):
                x = t[2 * j]
                y = t[2 * j + 1] if 2 * j + 1 < K else jnp.zeros_like(x)
                pair = jnp.concatenate([jnp.where(low, x, roll(y)), jnp.where(low, roll(x), y)], axis=0)
                op[r, :, pl.ds(j * LANES, LANES)] = split(pair)
        return carry

    lax.fori_loop(0, PAIRS, form, 0, unroll=2)

    def spread_halo(ref, side, q, carry):
        put_pair(side * 2 * BLK, q, ref[side, :, columns(q)])
        return carry

    def spread_halos(ref, halo):
        for p in range(PIECES):
            take(halo[p])
            for side in range(2):
                lax.fori_loop(
                    p * (PAIRS // PIECES), (p + 1) * (PAIRS // PIECES),
                    functools.partial(spread_halo, ref, side), 0, unroll=4,
                )

    spread_halos(halo0, halo)

    masks = half_masks()

    def product(out, q, carry):
        even = apply_row(stack, lidx_ref, op, 2 * q, masks)
        odd = apply_row(stack, lidx_ref, op, 2 * q + 1, masks)
        out[:, columns(q)] = jnp.where(low_lanes(even.shape), even, odd)
        return carry

    def products(out, halo, n):
        copies, gram = [], None
        for p in range(PIECES):
            lax.fori_loop(
                p * (PAIRS // PIECES), (p + 1) * (PAIRS // PIECES),
                functools.partial(product, out), 0, unroll=4,
            )
            copies.append(send_halo(out, halo, n, p))
            parts = gram_parts(out[:, piece(p)])
            part = dot(parts, parts, NT)
            gram = part if gram is None else gram + part
        return copies, pack(fold_gram(gram))

    halo, partial[0] = products(x1, halo1, 1)
    started += sum(halo, [])

    first = send_grp(partial.at[0], 0)
    grp_got[0, g] = partial[0]

    def own1(q, carry):
        put_pair(BLK, q, x1[:, columns(q)])
        return carry

    lax.fori_loop(0, PAIRS, own1, 0, unroll=4)
    spread_halos(halo1, halo)
    take(first)
    partial[1] = sum_grp(0)
    second = send_sub(partial.at[1], sub_got, sub_send, sub_recv, 0)
    sub_got[0, s] = partial[1]
    started += first + second

    halo, partial[2] = products(z, halo2, 2)
    started += sum(halo, [])
    third = send_grp(partial.at[2], 1)
    grp_got[1, g] = partial[2]

    take(second)
    inverse1 = inverse_factor(sum_sub(0) / total_rows)
    wide1 = wide(inverse1)

    take(third)
    partial[3] = sum_grp(1)
    fourth = send_sub(partial.at[3], sub_got, sub_send, sub_recv, 1)
    sub_got[1, s] = partial[3]
    started += third + fourth

    def own2(q, carry):
        x = times(wide1, split(z[:, columns(q)]))
        halves[:, columns(q)] = split(x)
        put_pair(BLK, q, x)
        return carry

    lax.fori_loop(0, PAIRS, own2, 0, unroll=4)

    def ext2(side, q, carry):
        put_pair(side * 2 * BLK, q, times(wide1, split(halo2[side, :, columns(q)])))
        return carry

    for p in range(PIECES):
        take(halo[p])
        for side in range(2):
            lax.fori_loop(
                p * (PAIRS // PIECES), (p + 1) * (PAIRS // PIECES),
                functools.partial(ext2, side), 0, unroll=4,
            )

    low, high = masks

    def project(q, carry):
        rows = []
        for r in (2 * q, 2 * q + 1):
            b = blocks_of(stack, lidx_ref, r)
            at = [lidx_ref[k, r] // BLK for k in range(K)]
            lefts = []
            for o in range(3):
                c = [(at[k] == o).astype(F32) for k in range(K)]
                m = [(low.astype(F32) * c[k] if k % 2 == 0 else high.astype(F32) * c[k]).astype(BF16) for k in range(K)]
                lefts.append(
                    jnp.concatenate([b[0] * m[0] + b[1] * m[1], b[2] * m[2] + b[3] * m[3], b[4] * m[4]], axis=1)
                )
            out = dot(jnp.concatenate(lefts, axis=0), op[r], NT)
            rows.append([fold(out[o * 2 * TS : (o + 1) * 2 * TS]) for o in range(3)])
        for o in range(3):
            x = jnp.where(low_lanes((TS, LANES)), rows[0][o], rows[1][o])
            mapped[o, :, columns(q)] = split(x)
        return carry

    lax.fori_loop(0, PAIRS, project, 0, unroll=4)
    h = [fold(dot(halves[...], mapped[o], NT)) for o in range(3)]
    is_first = (s == 0).astype(F32)
    is_last = (s == members - 1).astype(F32)
    term[0:HALF] = pack(is_first * h[0])
    term[HALF : 2 * HALF] = pack(h[1] + (1.0 - is_first) * h[0] + (1.0 - is_last) * h[2])
    term[2 * HALF : 3 * HALF] = pack(is_last * h[2])
    terms = [
        remote(term, final.at[s], term_send.at[i], term_recv.at[i], peer)
        for i, peer in enumerate(subs)
    ]
    for c in terms:
        c.start()
    final[s] = term[...]
    started += terms

    take(fourth)
    packed_gram = sum_sub(1) / total_rows
    square = inverse1[:, :TS]
    gram = jnp.concatenate([packed_gram[:, :TS], roll(packed_gram)[:, :TS]], axis=0)
    gram = exact(exact(square, gram, NN), square, NT)
    inverse_ref[...] = inverse_factor(jnp.concatenate([gram[:HALF], gram[HALF:]], axis=1))
    take(terms)
    acc = final[0]
    for i in range(1, members):
        acc = acc + final[i]
    acc_ref[...] = acc
    for c in started:
        c.wait_send()
    for c in [bulk(info_got, info_send, info_recv)] + [
        bulk(sent.at[k], tile_send.at[k], tile_recv.at[k]) for k in range(CAP)
    ]:
        c.wait_send()


def whole(owner, slot, nbr, shift, start, x, groups, members, total_rows):
    vmem = pl.BlockSpec(memory_space=pltpu.VMEM)
    dma = pltpu.SemaphoreType.DMA
    count = groups * members
    tiles = x.shape[2]
    return pl.pallas_call(
        functools.partial(whole_kernel, groups, members, total_rows),
        out_shape=(
            jax.ShapeDtypeStruct((2 * TS, ROWS), BF16),
            jax.ShapeDtypeStruct((TS, LANES), F32),
            jax.ShapeDtypeStruct((3 * HALF, LANES), F32),
        ),
        in_specs=[vmem, vmem, vmem, vmem, vmem, pl.BlockSpec(memory_space=pl.ANY)],
        out_specs=(vmem, vmem, vmem),
        scratch_shapes=[
            pltpu.VMEM((1, CAP * count), jnp.int32),
            pltpu.SMEM((1, CAP * count), jnp.int32),
            pltpu.VMEM((8, LANES), jnp.int32),
            pltpu.SMEM((8, LANES), jnp.int32),
            pltpu.VMEM((count, 1, LANES), F32),
            pltpu.VMEM((2, HALF * TS, tiles), F32),
            pltpu.VMEM((tiles, PITCH, LANES), F32),
            pltpu.VMEM((CAP, count, HALF, LANES), F32),
            pltpu.VMEM((CAP, (count + 1) * PITCH, LANES), F32),
            pltpu.VMEM((count, 1, LANES), F32),
            pltpu.VMEM(((HALF + 1) * DEPTH, LANES), F32),
            pltpu.VMEM((BLK, 2 * TS, 3 * LANES), BF16),
            pltpu.VMEM((TS, ROWS), F32),
            pltpu.VMEM((3 * BLK, 2 * TS, LANES), BF16),
            pltpu.VMEM((2, TS, ROWS), F32),
            pltpu.VMEM((2, TS, ROWS), F32),
            pltpu.VMEM((2, TS, ROWS), F32),
            pltpu.VMEM((TS, ROWS), F32),
            pltpu.VMEM((3, 2 * TS, ROWS), BF16),
            pltpu.VMEM((2, members, HALF, LANES), F32),
            pltpu.VMEM((2, groups, HALF, LANES), F32),
            pltpu.VMEM((4, HALF, LANES), F32),
            pltpu.VMEM((members, 3 * HALF, LANES), F32),
            pltpu.VMEM((3 * HALF, LANES), F32),
            dma((2,)),
            dma((2,)),
            dma((CAP,)),
            dma((CAP,)),
            dma,
            dma,
            dma((3, 2, PIECES)),
            dma((3, 2, PIECES)),
            dma((2, members - 1)),
            dma((2, members - 1)),
            dma((2, groups - 1)),
            dma((2, groups - 1)),
            dma((members - 1,)),
            dma((members - 1,)),
        ],
        compiler_params=pltpu.CompilerParams(
            collective_id=1, has_side_effects=True, vmem_limit_bytes=60 << 20
        ),
    )(owner, slot, nbr, shift, start, x)


def finish_kernel(groups, members, total_rows, halves_ref, inverse_ref, acc_ref, basis_ref, coarse_ref, tail):
    inverse = inverse_ref[...]
    step = pl.program_id(0)
    basis_ref[...] = times(wide(inverse), halves_ref[...])

    @pl.when(step == 0)
    def _():
        square = inverse[:, :TS]
        sides = []
        for o in range(3):
            packed = acc_ref[o * HALF : (o + 1) * HALF]
            sides.append(jnp.concatenate([packed, roll(packed)], axis=0))
        left = exact(square, jnp.concatenate(sides, axis=1), NN)
        left = jnp.concatenate([left[:, o * LANES : o * LANES + TS] for o in range(3)], axis=0)
        full = exact(left, square, NT) * (groups / total_rows)
        for o in range(3):
            tail[:, o * LANES : o * LANES + TS] = full[o * TS : (o + 1) * TS]
        each = TS // members
        mine = pl.ds(pl.multiple_of(lax.axis_index("sub") * each, each), each)
        for o in range(3):
            coarse_ref[:, o * TS : (o + 1) * TS] = tail[mine, o * LANES : o * LANES + TS]


def finish(halves, inverse, acc, groups, members, total_rows):
    steps = 2
    return pl.pallas_call(
        functools.partial(finish_kernel, groups, members, total_rows),
        out_shape=(
            jax.ShapeDtypeStruct((TS, ROWS), F32),
            jax.ShapeDtypeStruct((TS // members, 3 * TS), F32),
        ),
        grid=(steps,),
        in_specs=[
            pl.BlockSpec((2 * TS, ROWS // steps), lambda i: (0, i)),
            pl.BlockSpec((TS, LANES), lambda i: (0, 0)),
            pl.BlockSpec((3 * HALF, LANES), lambda i: (0, 0)),
        ],
        out_specs=(
            pl.BlockSpec((TS, ROWS // steps), lambda i: (0, i)),
            pl.BlockSpec((TS // members, 3 * TS), lambda i: (0, 0)),
        ),
        scratch_shapes=[pltpu.VMEM((TS, 3 * LANES), F32)],
    )(halves, inverse, acc)


def shards(tiles, owner, slot, nbr, shift, start):
    groups, members = lax.axis_size("grp"), lax.axis_size("sub")
    total_rows = float(ROWS * groups * members)
    count = tiles.shape[0]
    x = tiles.transpose(1, 2, 0).reshape(2, HALF * TS, count)
    halves, inverse, acc = whole(
        owner.T, slot.reshape(1, count), nbr.T, shift.reshape(PAIRS, LANES), start.T, x,
        groups, members, total_rows,
    )
    basis, coarse = finish(halves, inverse, acc, groups, members, total_rows)
    return basis.T, coarse[None]


def solution(mesh):
    placed = (
        P(("grp", "sub"), None, None),
        P(("grp", "sub"), None),
        P(("grp", "sub")),
        P(("grp", "sub"), None),
        P(("grp", "sub")),
        P(("grp", "sub"), None),
    )
    return jax.shard_map(
        shards,
        mesh=mesh,
        in_specs=placed,
        out_specs=(P(("grp", "sub"), None), P("grp", "sub", None)),
        check_vma=False,
    )
```
